1024 devices in a mesh: dp: 2 (over core), expert: 64 (over x, z), etp: 8 (over y).
Axes of the slice: x: 4, y: 8, z: 16, core: 2. Of those that a mesh axis runs over, the one named last changes fastest.
Arguments:
- tokens: bfloat16 [4096, 4096], P(('dp', 'expert')), may hold values from -6 to 6
- cotangent: bfloat16 [4096, 4096], P(('dp', 'expert')), may hold values from -6 to 6
- expert_ids: int32 [4096, 8], P(('dp', 'expert')), may hold values from 0 to 63, all different within a row; in each aligned block of 32 rows (0 to 31, 32 to 63, ...) at most 5 rows name the same one
- probs: bfloat16 [4096, 8], P(('dp', 'expert')), may hold values from 0.049804688 to 1
- gate_weight: bfloat16 [64, 4096, 1024], P('expert', 'dp', 'etp'), may hold values from -0.09375 to 0.09375
- up_weight: bfloat16 [64, 4096, 1024], P('expert', 'dp', 'etp'), may hold values from -0.09375 to 0.09375
- down_weight: bfloat16 [64, 4096, 1024], P('expert', 'dp', 'etp'), may hold values from -0.1875 to 0.1875
Outputs:
- d_tokens: bfloat16 [4096, 4096], P(('dp', 'expert'), 'etp')
- grad_gate: bfloat16 [64, 4096, 1024], P('expert', 'dp', 'etp')
- grad_up: bfloat16 [64, 4096, 1024], P('expert', 'dp', 'etp')
- grad_down: bfloat16 [64, 4096, 1024], P('expert', 'dp', 'etp')
The draws below stay inside these ranges and needn't reach their ends.
Inputs may be any that keep to these rules, and one draw needn't show every extreme that they name: `expert_ids`: each row names 8 different experts. Among the 32 rows of one index pair of dp and expert (aligned blocks), no expert is named by more than 5 rows, a bound that some block reaches.
All inputs are finite; a program needn't handle non-finite values.
Results may differ from the reference program's by a relative error of at most 0.02.
Values may be sent and summed in bfloat16 or wider, within the bound.
No kernel may reach another device: no remote copies, remote signals or barrier semaphores. Data moves between devices by JAX's collectives and lax.ppermute only.
A program may use at most 64 MiB of HBM per device.

```python
import math
import jax
import jax.numpy as jnp
import numpy as np
from jax import lax

D = 4096
FF = 1024
TOK_DEV = 32
EXPERTS = 64
TOPK = 8
CAP = 5
TOKENS = 4096
N_DP = 2
N_EXPERT = 64
N_ETP = 8


def block_scale(rng, dims, pieces, smallest, high):
    def one(dim, shards_of):
        heights = jax.random.uniform(jax.random.fold_in(jax.random.fold_in(rng, 6), dim), (shards_of,), jnp.float32, smallest / len(pieces), high / len(pieces))
        return jnp.repeat(jnp.exp(heights), dims[dim] // shards_of).reshape((-1,) + (1,) * (len(dims) - dim - 1))

    level = one(*pieces[0])
    for cut in pieces[1:]:
        level = level * one(*cut)
    return level


def shared_out(own_key, own, number, rows, amount, top, reach, slope):
    ranking = jax.random.permutation(own_key, amount)
    crowded, ordinary = load_shares(amount, rows * top, reach, slope, True), load_shares(amount, rows * top, reach, slope, False)
    places = jnp.arange(amount)

    def named(tallies, offset_by):
        used = int((tallies > 0).sum())
        fixed = max(1, used // 4)
        shifted = fixed + (places - fixed + offset_by * (used - fixed)) % max(1, amount - fixed)
        return jnp.zeros((amount,), jnp.int32).at[ranking[jnp.where(places < fixed, places, shifted)]].set(jnp.asarray(tallies, jnp.int32))

    tallies = jnp.where(number % 4 == 0, named(crowded, number // 4), named(ordinary, number - number // 4 - 1))
    mixed = jax.random.permutation(jax.random.fold_in(own, 3), amount)
    source_of, receiver = mixed[0:amount // 2 * 2:2], mixed[1:amount // 2 * 2:2]
    slack = jnp.minimum(tallies[source_of] - 1, reach - tallies[receiver]) // 2
    slack = jnp.where((source_of == ranking[0]) | (receiver == ranking[0]) | (tallies[receiver] == 0), 0, jnp.maximum(slack, 0))
    shifted = jax.random.randint(jax.random.fold_in(own, 4), (amount // 2,), 0, 1 << 20) % (slack + 1)
    tallies = tallies.at[source_of].add(-shifted).at[receiver].add(shifted)
    labels = jnp.searchsorted(jnp.cumsum(tallies), jnp.arange(rows * top), side="right").astype(jnp.int32)
    grid = labels.reshape(top, rows).T
    grid = grid[jax.random.permutation(jax.random.fold_in(own, 1), rows)]
    offset_by = jax.random.randint(jax.random.fold_in(own, 2), (rows, 1), 0, top)
    return jnp.take_along_axis(grid, (jnp.arange(top)[None, :] + offset_by) % top, axis=1)


def load_shares(count, total, bound, slope, full):
    portions = [(1 << 20) // math.isqrt(standing ** slope) + 1 for standing in range(1, count + 1)]
    largest = bound if full else min(bound, max(-(-total // count), total * portions[0] // sum(portions)))
    least = 1 if total - largest >= count - 1 else 0
    given, rest = [largest] + [least] * (count - 1), total - largest - least * (count - 1)
    while rest > 0:
        candidates = [i for i in range(1, count) if given[i] < largest] or [i for i in range(1, count) if given[i] < bound]
        whole, left = sum([portions[i] for i in candidates]), rest
        for i in candidates:
            extra = min(bound - given[i], max(1, left * portions[i] // whole), rest)
            given[i] = given[i] + extra
            rest = rest - extra
    return np.array(given)


def bell_draw(own_key, shape, spread, bound, cuts=(), kind=jnp.bfloat16):
    array = spread * jax.random.normal(own_key, shape, jnp.float32)
    if cuts:
        array = array * block_scale(own_key, shape, cuts, -0.22, 0.18)
    return jnp.clip(array, -bound, bound).astype(kind)


def setup_inputs(seed: int = 0) -> dict:
    arg_keys = jax.random.split(jax.random.key(seed), 8)
    tokens = bell_draw(arg_keys[0], (TOKENS, D), 1.0, 6.0, ((0, 128),))
    cotangent = bell_draw(arg_keys[1], (TOKENS, D), 1.0, 6.0, ((0, 128),))
    expert_ids_keys = jax.random.split(jax.random.fold_in(arg_keys[2], 1), TOKENS // TOK_DEV)
    expert_ids_turns = jax.random.permutation(jax.random.fold_in(arg_keys[2], 3), TOKENS // TOK_DEV)
    expert_ids = jax.vmap(lambda own, number: shared_out(jax.random.fold_in(arg_keys[2], 2), own, number, TOK_DEV, EXPERTS, TOPK, CAP, 2))(expert_ids_keys, expert_ids_turns).reshape((TOKENS, TOPK))
    probs = jnp.clip(jnp.exp(math.log(1.0) - 2.9996462 * jax.random.uniform(arg_keys[3], (TOKENS, TOPK), jnp.float32) ** block_scale(arg_keys[3], (TOKENS, TOPK), ((0, 128),), -0.2, 0.2)), 0.049804688, 1.0).astype(jnp.bfloat16)
    gate_weight = bell_draw(arg_keys[4], (EXPERTS, D, FF), D ** -0.5, 0.09375, ((0, 64), (1, 2), (2, 8)))
    up_weight = bell_draw(arg_keys[5], (EXPERTS, D, FF), D ** -0.5, 0.09375, ((0, 64), (1, 2), (2, 8)))
    down_weight = bell_draw(arg_keys[6], (EXPERTS, D, FF), FF ** -0.5, 0.1875, ((0, 64), (1, 2), (2, 8)))
    return {"tokens": tokens, "cotangent": cotangent, "expert_ids": expert_ids, "probs": probs, "gate_weight": gate_weight, "up_weight": up_weight, "down_weight": down_weight}


def route_slots(ids):
    onehot = (ids[..., None] == jnp.arange(EXPERTS, dtype=jnp.int32)).astype(jnp.int32)
    counts = lax.optimization_barrier(jnp.sum(onehot, axis=2))
    before = jnp.cumsum(counts, axis=1) - counts
    return lax.optimization_barrier(jnp.sum(onehot * before[:, :, None, :], axis=3)).astype(jnp.int32)

def half_grad(left, right):
    parts = jnp.einsum('nrd,nrf->ndf', left.astype(jnp.float32), right.astype(jnp.float32)).astype(jnp.bfloat16)
    return lax.optimization_barrier(jnp.sum(parts.astype(jnp.float32), axis=0)).astype(jnp.bfloat16)

def expert_step(packed):
    xs, dys, ps, w_gate, w_up, w_down = packed
    rows = xs.reshape(-1, D)
    gate = jnp.dot(rows, w_gate, preferred_element_type=jnp.float32)
    up = jnp.dot(rows, w_up, preferred_element_type=jnp.float32)
    sig = jax.nn.sigmoid(gate)
    act = gate * sig
    hidden = (act * up).astype(jnp.bfloat16)
    scaled = (ps.reshape(-1, 1).astype(jnp.float32) * dys.reshape(-1, D).astype(jnp.float32)).astype(jnp.bfloat16)
    d_hidden = jnp.dot(scaled, w_down, preferred_element_type=jnp.float32)
    d_up = (d_hidden * act).astype(jnp.bfloat16)
    d_gate = (d_hidden * up * sig * (1.0 + gate * (1.0 - sig))).astype(jnp.bfloat16)
    block = FF // N_ETP
    dg_blocks = d_gate.reshape(-1, N_ETP, block).astype(jnp.float32)
    du_blocks = d_up.reshape(-1, N_ETP, block).astype(jnp.float32)
    wg_blocks = w_gate.reshape(D, N_ETP, block).astype(jnp.float32)
    wu_blocks = w_up.reshape(D, N_ETP, block).astype(jnp.float32)
    parts = (jnp.einsum('rbf,dbf->brd', dg_blocks, wg_blocks) + jnp.einsum('rbf,dbf->brd', du_blocks, wu_blocks)).astype(jnp.bfloat16)
    d_rows = lax.optimization_barrier(jnp.sum(parts.astype(jnp.float32), axis=0)).astype(jnp.bfloat16)
    halves = N_EXPERT * CAP
    left = rows.reshape(N_DP, halves, D)
    left_scaled = scaled.reshape(N_DP, halves, D)
    grad_gate = half_grad(left, d_gate.reshape(N_DP, halves, FF))
    grad_up = half_grad(left, d_up.reshape(N_DP, halves, FF))
    grad_down = half_grad(left_scaled, hidden.reshape(N_DP, halves, FF))
    return (d_rows.reshape(xs.shape), grad_gate, grad_up, grad_down)

def reference(tokens, cotangent, expert_ids, probs, gate_weight, up_weight, down_weight):
    groups = N_DP * N_EXPERT
    ids = expert_ids.reshape(groups, TOK_DEV, TOPK)
    slots = route_slots(ids)
    dest = ids * CAP + slots
    places = (dest[..., None] == jnp.arange(EXPERTS * CAP, dtype=jnp.int32)).astype(jnp.float32)
    occupied = lax.optimization_barrier(jnp.sum(places, axis=2))
    prob_rows = probs.reshape(groups, TOK_DEV, TOPK).astype(jnp.float32)
    xs = tokens.reshape(groups, TOK_DEV, D).astype(jnp.float32)
    dys = cotangent.reshape(groups, TOK_DEV, D).astype(jnp.float32)
    x_buf = jnp.einsum('gts,gtd->gsd', occupied, xs, precision=lax.Precision.HIGHEST).astype(jnp.bfloat16)
    dy_buf = jnp.einsum('gts,gtd->gsd', occupied, dys, precision=lax.Precision.HIGHEST).astype(jnp.bfloat16)
    p_buf = jnp.einsum('gtks,gtk->gs', places, prob_rows, precision=lax.Precision.HIGHEST).astype(jnp.bfloat16)
    x_exp = jnp.moveaxis(x_buf.reshape(groups, EXPERTS, CAP, D), 1, 0)
    dy_exp = jnp.moveaxis(dy_buf.reshape(groups, EXPERTS, CAP, D), 1, 0)
    p_exp = jnp.moveaxis(p_buf.reshape(groups, EXPERTS, CAP), 1, 0)
    d_slots, grad_gate, grad_up, grad_down = lax.map(expert_step, (x_exp, dy_exp, p_exp, gate_weight, up_weight, down_weight))
    group_index = jnp.arange(groups, dtype=jnp.int32)[:, None, None]
    picked = d_slots[ids, group_index, slots]
    d_tokens = lax.optimization_barrier(jnp.sum(prob_rows[..., None] * picked.astype(jnp.float32), axis=2)).astype(jnp.bfloat16)
    return (d_tokens.reshape(TOKENS, D), grad_gate, grad_up, grad_down)
```

```python
import jax
import jax.numpy as jnp
from jax import lax
from jax.experimental import pallas as pl
from jax.experimental.pallas import tpu as pltpu
from jax.sharding import Mesh
from jax.sharding import PartitionSpec as P

F32 = jnp.float32
BF16 = jnp.bfloat16
LANES = 128


def pack_kernel(capacity, ids_ref, probs_ref, x_ref, dy_ref, out_ref, table_ref, flat):
    choose, tok = ids_ref.shape
    rows = table_ref.shape[0]
    experts = rows // capacity
    width = x_ref.shape[1]
    chunks = width // LANES
    expert = lax.broadcasted_iota(jnp.int32, (experts, tok), 0)
    named = [expert == ids_ref[k : k + 1, :] for k in range(choose)]
    counts = sum(m.astype(F32) for m in named)
    earlier = lax.broadcasted_iota(jnp.int32, (tok, tok), 0) < lax.broadcasted_iota(
        jnp.int32, (tok, tok), 1
    )
    before = jnp.dot(
        counts.astype(BF16), earlier.astype(F32).astype(BF16), preferred_element_type=F32
    )
    row = lax.broadcasted_iota(jnp.int32, (rows, tok), 0)
    occupied = jnp.zeros((rows, tok), F32)
    weights = jnp.zeros((rows, tok), F32)
    for k in range(choose):
        slot = jnp.sum(jnp.where(named[k], before, 0.0), axis=0, keepdims=True)
        dest = ids_ref[k : k + 1, :] * capacity + slot.astype(jnp.int32)
        here = row == dest
        occupied = jnp.where(here, 1.0, occupied)
        weights = jnp.where(here, probs_ref[k : k + 1, :].astype(F32), weights)
    table = weights.astype(BF16)
    table_ref[...] = table
    placed = jnp.dot(occupied.astype(BF16), x_ref[...], preferred_element_type=F32)
    scaled = jnp.dot(table, dy_ref[...], preferred_element_type=F32)
    for c in range(chunks):
        cols = slice(c * LANES, (c + 1) * LANES)
        flat[pl.ds(c, rows, stride=2 * chunks), :] = placed[:, cols]
        flat[pl.ds(chunks + c, rows, stride=2 * chunks), :] = scaled[:, cols]
    out_ref[...] = flat[...].astype(BF16)


def pack(ids, probs, tokens, cotangent, column, width, rows, capacity):
    tok = tokens.shape[0]
    height = rows * 2 * (width // LANES)
    whole = pl.BlockSpec(memory_space=pltpu.VMEM)
    return pl.pallas_call(
        lambda col, *refs: pack_kernel(capacity, *refs),
        grid_spec=pltpu.PrefetchScalarGridSpec(
            num_scalar_prefetch=1,
            grid=(1,),
            in_specs=[
                whole,
                whole,
                pl.BlockSpec((tok, width), lambda i, col: (0, col[0])),
                pl.BlockSpec((tok, width), lambda i, col: (0, col[0])),
            ],
            out_specs=[whole, whole],
            scratch_shapes=[pltpu.VMEM((height, LANES), F32)],
        ),
        out_shape=[
            jax.ShapeDtypeStruct((height, LANES), BF16),
            jax.ShapeDtypeStruct((rows, tok), BF16),
        ],
        compiler_params=pltpu.CompilerParams(vmem_limit_bytes=32 << 20),
        name="pack",
    )(column, ids, probs, tokens, cotangent)


def unpack_kernel(flat_ref, x_ref, dy_ref, flat):
    rows, width = x_ref.shape
    chunks = width // LANES
    flat[...] = flat_ref[...].astype(F32)
    for c in range(chunks):
        cols = slice(c * LANES, (c + 1) * LANES)
        x_ref[:, cols] = flat[pl.ds(c, rows, stride=2 * chunks), :].astype(BF16)
        dy_ref[:, cols] = flat[pl.ds(chunks + c, rows, stride=2 * chunks), :].astype(BF16)


def unpack(flat, rows, width):
    whole = pl.BlockSpec(memory_space=pltpu.VMEM)
    return pl.pallas_call(
        unpack_kernel,
        in_specs=[whole],
        out_specs=[whole, whole],
        scratch_shapes=[pltpu.VMEM(flat.shape, F32)],
        out_shape=[jax.ShapeDtypeStruct((rows, width), BF16)] * 2,
        compiler_params=pltpu.CompilerParams(vmem_limit_bytes=32 << 20),
        name="unpack",
    )(flat)


def shift(axis, step):
    n = lax.axis_size(axis)
    return [(i, (i + step) % n) for i in range(n)]


def ring(value, axis, rightward, leftward):
    held = {0: value}
    n = lax.axis_size(axis)
    right = left = value
    for s in range(1, max(rightward, leftward) + 1):
        if s <= rightward:
            right = lax.ppermute(right, axis, shift(axis, 1))
            held[s] = right
        if s <= leftward:
            left = lax.ppermute(left, axis, shift(axis, -1))
            held[n - s] = left
    return held


def shards(tokens, cotangent, expert_ids, probs, gate_weight, up_weight, down_weight):
    peers = ("x", "z")
    owners = lax.axis_size("x") * lax.axis_size("z")
    parts = lax.axis_size("y")
    core, place = lax.axis_index("dp"), lax.axis_index("y")
    tok, model = tokens.shape
    choose = expert_ids.shape[1]
    half = model // 2
    width = model // parts
    per_half = half // width
    hid = gate_weight.shape[2]
    capacity = min(tok, (5 * tok * choose + 4 * owners - 1) // (4 * owners))
    rows = owners * capacity

    swap = shift("dp", 1)
    gate_own, up_own, down_own = gate_weight[0], up_weight[0], down_weight[0]
    gate_other = lax.ppermute(gate_own, "dp", swap)
    up_other = lax.ppermute(up_own, "dp", swap)
    down_other = lax.ppermute(down_own, "dp", swap)
    first = core == 0

    flat, table = pack(
        expert_ids.T,
        probs.T,
        tokens,
        cotangent,
        place.astype(jnp.int32)[None],
        width,
        rows,
        capacity,
    )
    flat = lax.all_to_all(
        flat.reshape(owners, -1, LANES), peers, split_axis=0, concat_axis=0, tiled=True
    )

    low = jnp.where(first, gate_own, up_other)
    high = jnp.where(first, gate_other, up_own)
    turned = jnp.concatenate((low, high)).reshape(parts, width, hid)
    turned = lax.all_to_all(turned, "y", split_axis=0, concat_axis=0)
    turned_other = lax.ppermute(turned, "dp", swap)
    columns = jnp.concatenate(
        (jnp.where(first, turned, turned_other), jnp.where(first, turned_other, turned)), axis=2
    )

    both = jnp.concatenate(
        (
            jnp.concatenate((gate_own, up_own), axis=1),
            jnp.concatenate((gate_other, up_other), axis=1),
        )
    )
    down = jnp.concatenate((down_own, down_other))

    x_own, dy_own = unpack(flat.reshape(-1, LANES), rows, width)
    x_ring = ring(x_own, "y", parts // 2, parts // 2 - 1)
    dy_ring = ring(dy_own, "y", parts // 2 - 1, parts // 2)

    def block_of(distance):
        return lax.rem(place - distance + parts, parts)

    acc = jnp.zeros((rows, 2 * hid), F32)
    back = jnp.zeros((rows, hid), F32)
    for d in sorted(x_ring, key=lambda d: min(d, parts - d)):
        block = block_of(d)
        start = jnp.where(block // per_half == core, 0, half) + lax.rem(block, per_half) * width
        piece = lax.dynamic_slice_in_dim(both, start, width, 0)
        acc = acc + jnp.dot(x_ring[d], piece, preferred_element_type=F32)
        piece = lax.dynamic_slice_in_dim(down, start, width, 0)
        back = back + jnp.dot(dy_ring[d], piece, preferred_element_type=F32)
    gate, up = acc[:, :hid], acc[:, hid:]
    sig = jax.nn.sigmoid(gate)
    act = gate * sig
    hidden = (act * up).astype(BF16)
    d_up = (back * act).astype(BF16)
    d_gate = (back * up * sig * (1.0 + gate * (1.0 - sig))).astype(BF16)
    d_both = jnp.concatenate((d_gate, d_up), axis=1)

    d_ring = ring(d_both, "y", parts // 2, parts // 2 - 1)
    d_rows = jnp.zeros((rows, width), F32)
    for d in sorted(d_ring, key=lambda d: min(d, parts - d)):
        piece = lax.dynamic_index_in_dim(columns, block_of(d), 0, keepdims=False)
        d_rows = d_rows + lax.dot_general(
            d_ring[d], piece, (((1,), (1,)), ((), ())), preferred_element_type=F32
        )
    d_rows = d_rows.astype(BF16).reshape(owners, -1, LANES)
    returned = lax.all_to_all(d_rows, peers, split_axis=0, concat_axis=0, tiled=True)
    d_tokens = lax.dot_general(
        table,
        returned.reshape(rows, width),
        (((0,), (0,)), ((), ())),
        preferred_element_type=F32,
    ).astype(BF16)

    x_all = jnp.stack([x_ring[d] for d in range(parts)])
    dy_all = jnp.stack([dy_ring[d] for d in range(parts)])
    grads_both = jnp.einsum("prc,rf->pcf", x_all, d_both, preferred_element_type=F32).astype(BF16)
    grads_down = jnp.einsum("prc,rf->pcf", dy_all, hidden, preferred_element_type=F32).astype(BF16)
    grads = jnp.concatenate((grads_both, grads_down), axis=2)

    def of_half(which):
        order = lax.rem(place - which * per_half - jnp.arange(per_half) + 2 * parts, parts)
        return jnp.take(grads, order, axis=0).reshape(half, 3 * hid)

    received = lax.ppermute(of_half(1 - core), "dp", swap)
    total = (of_half(core).astype(F32) + received.astype(F32)).astype(BF16)
    return (
        d_tokens,
        total[None, :, :hid],
        total[None, :, hid : 2 * hid],
        total[None, :, 2 * hid :],
    )


def solution(mesh):
    dp, experts, etp = mesh.devices.shape
    inner = min(16, experts)
    grid = Mesh(mesh.devices.reshape(dp, experts // inner, inner, etp), ("dp", "x", "z", "y"))
    row = P(("dp", "x", "z"), None)
    weight = P(("x", "z"), "dp", "y")
    return jax.shard_map(
        shards,
        mesh=grid,
        in_specs=(row, row, row, row, weight, weight, weight),
        out_specs=(P(("dp", "x", "z"), "y"), weight, weight, weight),
        check_vma=False,
    )
```

```python
import jax
import jax.numpy as jnp
from jax import lax
from jax.experimental import pallas as pl
from jax.experimental.pallas import tpu as pltpu
from jax.sharding import Mesh
from jax.sharding import PartitionSpec as P

F32 = jnp.float32
BF16 = jnp.bfloat16
LANES = 128


def pack_kernel(capacity, ids_ref, probs_ref, x_ref, dy_ref, out_ref, table_ref, flat):
    choose, tok = ids_ref.shape
    rows = table_ref.shape[0]
    experts = rows // capacity
    width = x_ref.shape[1]
    chunks = width // LANES
    expert = lax.broadcasted_iota(jnp.int32, (experts, tok), 0)
    named = [expert == ids_ref[k : k + 1, :] for k in range(choose)]
    counts = sum(m.astype(F32) for m in named)
    earlier = lax.broadcasted_iota(jnp.int32, (tok, tok), 0) < lax.broadcasted_iota(
        jnp.int32, (tok, tok), 1
    )
    before = jnp.dot(
        counts.astype(BF16), earlier.astype(F32).astype(BF16), preferred_element_type=F32
    )
    row = lax.broadcasted_iota(jnp.int32, (rows, tok), 0)
    occupied = jnp.zeros((rows, tok), F32)
    weights = jnp.zeros((rows, tok), F32)
    for k in range(choose):
        slot = jnp.sum(jnp.where(named[k], before, 0.0), axis=0, keepdims=True)
        dest = ids_ref[k : k + 1, :] * capacity + slot.astype(jnp.int32)
        here = row == dest
        occupied = jnp.where(here, 1.0, occupied)
        weights = jnp.where(here, probs_ref[k : k + 1, :].astype(F32), weights)
    table = weights.astype(BF16)
    table_ref[...] = table
    placed = jnp.dot(occupied.astype(BF16), x_ref[...], preferred_element_type=F32)
    scaled = jnp.dot(table, dy_ref[...], preferred_element_type=F32)
    for c in range(chunks):
        cols = slice(c * LANES, (c + 1) * LANES)
        flat[pl.ds(c, rows, stride=2 * chunks), :] = placed[:, cols]
        flat[pl.ds(chunks + c, rows, stride=2 * chunks), :] = scaled[:, cols]
    out_ref[...] = flat[...].astype(BF16)


def pack(ids, probs, tokens, cotangent, column, width, rows, capacity):
    tok = tokens.shape[0]
    height = rows * 2 * (width // LANES)
    whole = pl.BlockSpec(memory_space=pltpu.VMEM)
    return pl.pallas_call(
        lambda col, *refs: pack_kernel(capacity, *refs),
        grid_spec=pltpu.PrefetchScalarGridSpec(
            num_scalar_prefetch=1,
            grid=(1,),
            in_specs=[
                whole,
                whole,
                pl.BlockSpec((tok, width), lambda i, col: (0, col[0])),
                pl.BlockSpec((tok, width), lambda i, col: (0, col[0])),
            ],
            out_specs=[whole, whole],
            scratch_shapes=[pltpu.VMEM((height, LANES), F32)],
        ),
        out_shape=[
            jax.ShapeDtypeStruct((height, LANES), BF16),
            jax.ShapeDtypeStruct((rows, tok), BF16),
        ],
        compiler_params=pltpu.CompilerParams(vmem_limit_bytes=60 << 20),
        name="pack",
    )(column, ids, probs, tokens, cotangent)


def unpack_kernel(flat_ref, out_ref, flat):
    rows, width = out_ref.shape
    chunks = width // LANES
    flat[...] = flat_ref[...].astype(F32)
    for c in range(chunks):
        cols = slice(c * LANES, (c + 1) * LANES)
        out_ref[:, cols] = flat[pl.ds(c, rows, stride=chunks), :].astype(BF16)


def unpack(flat, rows, width):
    whole = pl.BlockSpec(memory_space=pltpu.VMEM)
    return pl.pallas_call(
        unpack_kernel,
        in_specs=[whole],
        out_specs=whole,
        scratch_shapes=[pltpu.VMEM(flat.shape, F32)],
        out_shape=jax.ShapeDtypeStruct((rows, width), BF16),
        compiler_params=pltpu.CompilerParams(vmem_limit_bytes=16 << 20),
        name="unpack",
    )(flat)


def transposed_dot(left, right):
    return lax.dot_general(left, right, (((0,), (0,)), ((), ())), preferred_element_type=F32)


def grads_kernel(parts, position, *refs):
    blocks, (x_mid, dy_mid, both_ref, hidden_ref, out_ref) = refs[: parts - 1], refs[parts - 1 :]
    place, wanted = position[0], position[1]
    width = x_mid.shape[1]
    hid = hidden_ref.shape[1]
    per_half = parts // 2
    for d in range(parts):
        source = lax.rem(place - d + parts, parts)

        @pl.when(source // per_half == wanted)
        def _():
            if d == parts // 2:
                x, dy = x_mid[...], dy_mid[...]
            else:
                block = blocks[d if d < parts // 2 else d - 1]
                x, dy = block[:, :width], block[:, width:]
            into = pl.ds(pl.multiple_of(lax.rem(source, per_half) * width, width), width)
            out_ref[into, : 2 * hid] = transposed_dot(x, both_ref[...]).astype(BF16)
            out_ref[into, 2 * hid :] = transposed_dot(dy, hidden_ref[...]).astype(BF16)


def grads(place, which, blocks, x_mid, dy_mid, both, hidden):
    parts = len(blocks) + 1
    half = parts // 2 * x_mid.shape[1]
    whole = pl.BlockSpec(memory_space=pltpu.VMEM)
    out = jax.ShapeDtypeStruct((half, both.shape[1] + hidden.shape[1]), BF16)
    return pl.pallas_call(
        lambda *refs: grads_kernel(parts, *refs),
        in_specs=[pl.BlockSpec(memory_space=pltpu.SMEM)] + [whole] * (parts + 3),
        out_specs=whole,
        out_shape=out,
        cost_estimate=pl.CostEstimate(
            flops=2 * both.shape[0] * half * out.shape[1], bytes_accessed=8 << 20, transcendentals=0
        ),
        compiler_params=pltpu.CompilerParams(vmem_limit_bytes=16 << 20),
        name="grads",
    )(jnp.stack((place, which)).astype(jnp.int32), *blocks, x_mid, dy_mid, both, hidden)


def shift(axis, step):
    n = lax.axis_size(axis)
    return [(i, (i + step) % n) for i in range(n)]


def shards(tokens, cotangent, expert_ids, probs, gate_weight, up_weight, down_weight):
    peers = ("x", "z")
    owners = lax.axis_size("x") * lax.axis_size("z")
    parts = lax.axis_size("y")
    middle = parts // 2
    core, place = lax.axis_index("dp"), lax.axis_index("y")
    tok, model = tokens.shape
    choose = expert_ids.shape[1]
    half = model // 2
    width = model // parts
    per_half = half // width
    hid = gate_weight.shape[2]
    capacity = min(tok, (5 * tok * choose + 4 * owners - 1) // (4 * owners))
    rows = owners * capacity
    first = core == 0
    swap = shift("dp", 1)

    def block_of(distance):
        return lax.rem(place - distance + 2 * parts, parts)

    flat, table = pack(
        expert_ids.T,
        probs.T,
        tokens,
        cotangent,
        place.astype(jnp.int32)[None],
        width,
        rows,
        capacity,
    )
    flat = lax.all_to_all(
        flat.reshape(owners, -1, LANES), peers, split_axis=0, concat_axis=0, tiled=True
    )

    gate_own, up_own, down_own = gate_weight[0], up_weight[0], down_weight[0]
    gate_other = lax.ppermute(gate_own, "dp", swap)
    up_other = lax.ppermute(up_own, "dp", swap)
    down_other = lax.ppermute(down_own, "dp", swap)

    low = jnp.where(first, gate_own, up_other)
    high = jnp.where(first, gate_other, up_own)
    turn = jnp.concatenate((low, high)).reshape(parts, width, hid)
    turned = []
    for d in range(parts):
        piece = lax.dynamic_index_in_dim(turn, block_of(-d), 0, keepdims=False)
        turned.append(lax.ppermute(piece, "y", shift("y", d)) if d else piece)
    turned_other = lax.ppermute(jnp.concatenate(turned), "dp", swap)

    both = jnp.concatenate(
        (
            jnp.concatenate((gate_own, up_own), axis=1),
            jnp.concatenate((gate_other, up_other), axis=1),
        )
    )
    down = jnp.concatenate((down_own, down_other))
    flat, turned, turned_other, both, down = lax.optimization_barrier(
        (flat, turned, turned_other, both, down)
    )

    own = unpack(flat.reshape(-1, LANES), rows, 2 * width)
    blocks = {0: own}
    right = left = own
    for d in range(1, middle):
        right = lax.ppermute(right, "y", shift("y", 1))
        left = lax.ppermute(left, "y", shift("y", -1))
        blocks[d], blocks[parts - d] = right, left
    x_mid = lax.ppermute(right[:, :width], "y", shift("y", 1))
    dy_mid = lax.ppermute(left[:, width:], "y", shift("y", -1))

    acc = jnp.zeros((rows, 2 * hid), F32)
    back = jnp.zeros((rows, hid), F32)
    near = sorted(range(parts), key=lambda d: min(d, parts - d))
    for d in near:
        x, dy = (x_mid, dy_mid) if d == middle else (blocks[d][:, :width], blocks[d][:, width:])
        block = block_of(d)
        start = jnp.where(block // per_half == core, 0, half) + lax.rem(block, per_half) * width
        piece = lax.dynamic_slice_in_dim(both, start, width, 0)
        acc = acc + jnp.dot(x, piece, preferred_element_type=F32)
        piece = lax.dynamic_slice_in_dim(down, start, width, 0)
        back = back + jnp.dot(dy, piece, preferred_element_type=F32)
    gate, up = acc[:, :hid], acc[:, hid:]
    sig = jax.nn.sigmoid(gate)
    act = gate * sig
    hidden = (act * up).astype(BF16)
    d_up = (back * act).astype(BF16)
    d_gate = (back * up * sig * (1.0 + gate * (1.0 - sig))).astype(BF16)
    d_both = jnp.concatenate(
        (jnp.where(first, d_gate, d_up), jnp.where(first, d_up, d_gate)), axis=1
    )

    d_ring = {0: d_both}
    right = left = d_both
    for d in range(1, middle + 1):
        right = lax.ppermute(right, "y", shift("y", 1))
        d_ring[d] = right
        if d < middle:
            left = lax.ppermute(left, "y", shift("y", -1))
            d_ring[parts - d] = left
    d_rows = jnp.zeros((rows, width), F32)
    contract = (((1,), (1,)), ((), ()))
    for d in near:
        other = turned_other[d * width : (d + 1) * width]
        d_rows = d_rows + lax.dot_general(
            d_ring[d][:, :hid], turned[d], contract, preferred_element_type=F32
        )
        d_rows = d_rows + lax.dot_general(
            d_ring[d][:, hid:], other, contract, preferred_element_type=F32
        )
    d_rows = d_rows.astype(BF16).reshape(owners, -1, LANES)
    operands = (
        [blocks[d] for d in range(parts) if d != middle],
        x_mid,
        dy_mid,
        jnp.concatenate((d_gate, d_up), axis=1),
        hidden,
    )
    received = lax.ppermute(grads(place, 1 - core, *operands), "dp", swap)
    d_rows, operands = lax.optimization_barrier((d_rows, operands))
    returned = lax.all_to_all(d_rows, peers, split_axis=0, concat_axis=0, tiled=True)
    d_tokens = transposed_dot(table, returned.reshape(rows, width)).astype(BF16)
    mine = grads(place, core, *operands)
    total = (mine.astype(F32) + received.astype(F32)).astype(BF16)
    return (
        d_tokens,
        total[None, :, :hid],
        total[None, :, hid : 2 * hid],
        total[None, :, 2 * hid :],
    )


def solution(mesh):
    dp, experts, etp = mesh.devices.shape
    inner = min(16, experts)
    grid = Mesh(mesh.devices.reshape(dp, experts // inner, inner, etp), ("dp", "x", "z", "y"))
    row = P(("dp", "x", "z"), None)
    weight = P(("x", "z"), "dp", "y")
    return jax.shard_map(
        shards,
        mesh=grid,
        in_specs=(row, row, row, row, weight, weight, weight),
        out_specs=(P(("dp", "x", "z"), "y"), weight, weight, weight),
        check_vma=False,
    )
```

```python
import jax
import jax.numpy as jnp
from jax import lax
from jax.experimental import pallas as pl
from jax.experimental.pallas import tpu as pltpu
from jax.sharding import Mesh
from jax.sharding import PartitionSpec as P

F32 = jnp.float32
BF16 = jnp.bfloat16
LANES = 128
TILE = 8


def whole(shape):
    return pl.BlockSpec(
        shape, lambda *_: (0,) * len(shape), pipeline_mode=pl.Buffered(buffer_count=1)
    )


def local_call(kernel, name, scalars, operands, outs, scratch=(), flops=0, vmem=24):
    out_specs = jax.tree.map(lambda o: whole(o.shape), outs)
    return pl.pallas_call(
        kernel,
        grid=(1,),
        in_specs=[pl.BlockSpec(memory_space=pltpu.SMEM)] + [whole(o.shape) for o in operands],
        out_specs=out_specs,
        out_shape=outs,
        scratch_shapes=list(scratch),
        cost_estimate=pl.CostEstimate(flops=flops, bytes_accessed=1 << 20, transcendentals=0),
        compiler_params=pltpu.CompilerParams(vmem_limit_bytes=vmem << 20),
        name=name,
    )(scalars, *operands)


def transposed_dot(left, right):
    return lax.dot_general(left, right, (((0,), (0,)), ((), ())), preferred_element_type=F32)


def shift(axis, step):
    n = lax.axis_size(axis)
    return [(i, (i + step) % n) for i in range(n)]


def pack_kernel(capacity, col, ids_ref, probs_ref, x_ref, dy_ref, out_ref, table_ref, flat):
    choose, tok = ids_ref.shape
    rows = table_ref.shape[0]
    experts = rows // capacity
    chunks = x_ref.shape[1] // LANES
    stretch = flat.shape[0] // experts
    expert = lax.broadcasted_iota(jnp.int32, (experts, tok), 0)
    named = [expert == ids_ref[k : k + 1, :] for k in range(choose)]
    counts = sum(m.astype(F32) for m in named)
    earlier = lax.broadcasted_iota(jnp.int32, (tok, tok), 0) < lax.broadcasted_iota(
        jnp.int32, (tok, tok), 1
    )
    before = jnp.dot(
        counts.astype(BF16), earlier.astype(F32).astype(BF16), preferred_element_type=F32
    )
    row = lax.broadcasted_iota(jnp.int32, (rows, tok), 0)
    occupied = jnp.zeros((rows, tok), F32)
    weights = jnp.zeros((rows, tok), F32)
    for k in range(choose):
        slot = jnp.sum(jnp.where(named[k], before, 0.0), axis=0, keepdims=True)
        here = row == slot.astype(jnp.int32) * experts + ids_ref[k : k + 1, :]
        occupied = jnp.where(here, 1.0, occupied)
        weights = jnp.where(here, probs_ref[k : k + 1, :].astype(F32), weights)
    table = weights.astype(BF16)
    table_ref[...] = table
    placed = jnp.dot(occupied.astype(BF16), x_ref[...], preferred_element_type=F32)
    scaled = jnp.dot(table, dy_ref[...], preferred_element_type=F32)
    for s in range(capacity):
        of = slice(s * experts, (s + 1) * experts)
        for c in range(chunks):
            cols = slice(c * LANES, (c + 1) * LANES)
            at = s * 2 * chunks + c
            flat[pl.ds(at, experts, stride=stretch), :] = placed[of, cols]
            flat[pl.ds(at + chunks, experts, stride=stretch), :] = scaled[of, cols]
    out_ref[...] = flat[...].astype(BF16)


def pack(ids, probs, tokens, cotangent, column, width, experts, capacity):
    tok = tokens.shape[0]
    rows = experts * capacity
    height = rows * 2 * (width // LANES)
    wide = pl.BlockSpec((tok, width), lambda i, col: (0, col[0]))
    return pl.pallas_call(
        lambda *refs: pack_kernel(capacity, *refs),
        grid_spec=pltpu.PrefetchScalarGridSpec(
            num_scalar_prefetch=1,
            grid=(1,),
            in_specs=[whole(ids.shape), whole(probs.shape), wide, wide],
            out_specs=[whole((height, LANES)), whole((rows, tok))],
            scratch_shapes=[pltpu.VMEM((height, LANES), F32)],
        ),
        out_shape=[
            jax.ShapeDtypeStruct((height, LANES), BF16),
            jax.ShapeDtypeStruct((rows, tok), BF16),
        ],
        compiler_params=pltpu.CompilerParams(vmem_limit_bytes=60 << 20),
        name="pack",
    )(column, ids, probs, tokens, cotangent)


def unpack_kernel(capacity, _, flat_ref, out_ref, flat):
    rows, width = out_ref.shape
    owners, chunks = rows // capacity, width // LANES
    stretch = flat.shape[0] // owners
    flat[...] = flat_ref[...].astype(F32)
    for s in range(capacity):
        for c in range(chunks):
            out_ref[s * owners : (s + 1) * owners, c * LANES : (c + 1) * LANES] = flat[
                pl.ds(s * chunks + c, owners, stride=stretch), :
            ].astype(BF16)


def weights_at(parts, distance, position, width, weights):
    place, core = position[0], position[1]
    per_half = parts // 2
    source = lax.rem(place - distance + parts, parts)
    of = pl.ds(pl.multiple_of(lax.rem(source, per_half) * width, width), width)
    mine = source // per_half == core
    return jnp.concatenate(
        [
            jnp.where(mine, own[of, :], other[of, :])
            for own, other in zip(weights[::2], weights[1::2])
        ],
        axis=1,
    )


def forward_most(parts, distances, middle, position, *refs):
    blocks, weights = refs[: len(distances)], refs[len(distances) : -2]
    out, mid_ref = refs[-2:]
    rows, width = blocks[0].shape[0], blocks[0].shape[1] // 2
    hid = out.shape[1] // 3
    acc, back = jnp.zeros((rows, 2 * hid), F32), jnp.zeros((rows, hid), F32)
    for d, block in zip(distances, blocks):
        piece = weights_at(parts, d, position, width, weights)
        acc = acc + jnp.dot(block[:, :width], piece[:, : 2 * hid], preferred_element_type=F32)
        back = back + jnp.dot(block[:, width:], piece[:, 2 * hid :], preferred_element_type=F32)
    out[:, : 2 * hid] = acc
    out[:, 2 * hid :] = back
    mid_ref[...] = weights_at(parts, middle, position, width, weights)


def forward_last(position, x_ref, dy_ref, piece_ref, begun, ordered_ref, both_ref, hidden_ref):
    hid = hidden_ref.shape[1]
    acc = begun[:, : 2 * hid] + jnp.dot(
        x_ref[...], piece_ref[:, : 2 * hid], preferred_element_type=F32
    )
    back = begun[:, 2 * hid :] + jnp.dot(
        dy_ref[...], piece_ref[:, 2 * hid :], preferred_element_type=F32
    )
    gate, up = acc[:, :hid], acc[:, hid:]
    sig = 1.0 / (1.0 + jnp.exp(-gate))
    act = gate * sig
    hidden_ref[...] = (act * up).astype(BF16)
    d_up = back * act
    d_gate = back * up * sig * (1.0 + gate * (1.0 - sig))
    both_ref[:, :hid] = d_gate.astype(BF16)
    both_ref[:, hid:] = d_up.astype(BF16)
    first = position[1] == 0
    ordered_ref[:, :hid] = jnp.where(first, d_gate, d_up).astype(BF16)
    ordered_ref[:, hid:] = jnp.where(first, d_up, d_gate).astype(BF16)


def back_kernel(parts, capacity, _, *refs):
    blocks, turned = refs[:parts], refs[parts : 2 * parts]
    other_ref, out_ref, flat = refs[2 * parts :]
    rows, width = blocks[0].shape[0], turned[0].shape[0]
    owners, chunks = rows // capacity, width // LANES
    stretch = flat.shape[0] // owners
    total = jnp.zeros((rows, width), F32)
    for d in range(parts):
        weight = jnp.concatenate(
            (turned[d][...], other_ref[d * width : (d + 1) * width, :]), axis=1
        )
        total = total + lax.dot_general(
            blocks[d][...], weight, (((1,), (1,)), ((), ())), preferred_element_type=F32
        )
    for s in range(capacity):
        for c in range(chunks):
            flat[pl.ds(s * chunks + c, owners, stride=stretch), :] = total[
                s * owners : (s + 1) * owners, c * LANES : (c + 1) * LANES
            ]
    for pad in range(capacity * chunks, stretch):
        flat[pl.ds(pad, owners, stride=stretch), :] = jnp.zeros((owners, LANES), F32)
    out_ref[...] = flat[...].astype(BF16)


def combine_kernel(capacity, _, flat_ref, table_ref, out_ref, flat, rows_ref):
    rows, width = rows_ref.shape
    owners, chunks = rows // capacity, width // LANES
    stretch = flat.shape[0] // owners
    flat[...] = flat_ref[...].astype(F32)
    for s in range(capacity):
        for c in range(chunks):
            rows_ref[s * owners : (s + 1) * owners, c * LANES : (c + 1) * LANES] = flat[
                pl.ds(s * chunks + c, owners, stride=stretch), :
            ].astype(BF16)
    out_ref[...] = transposed_dot(table_ref[...], rows_ref[...]).astype(BF16)


def grads_kernel(parts, position, *refs):
    blocks, (x_mid, dy_mid, both_ref, hidden_ref, out_ref) = refs[: parts - 1], refs[parts - 1 :]
    place, wanted = position[0], position[1]
    width = x_mid.shape[1]
    hid = hidden_ref.shape[1]
    per_half = parts // 2
    for d in range(parts):
        source = lax.rem(place - d + parts, parts)

        @pl.when(source // per_half == wanted)
        def _():
            if d == parts // 2:
                x, dy = x_mid[...], dy_mid[...]
            else:
                block = blocks[d if d < parts // 2 else d - 1]
                x, dy = block[:, :width], block[:, width:]
            into = pl.ds(pl.multiple_of(lax.rem(source, per_half) * width, width), width)
            out_ref[into, : 2 * hid] = transposed_dot(x, both_ref[...]).astype(BF16)
            out_ref[into, 2 * hid :] = transposed_dot(dy, hidden_ref[...]).astype(BF16)


def grads(place, which, blocks, x_mid, dy_mid, both, hidden):
    parts = len(blocks) + 1
    half = parts // 2 * x_mid.shape[1]
    columns = both.shape[1] + hidden.shape[1]
    return local_call(
        lambda *refs: grads_kernel(parts, *refs),
        "grads",
        jnp.stack((place, which)).astype(jnp.int32),
        (*blocks, x_mid, dy_mid, both, hidden),
        jax.ShapeDtypeStruct((half, columns), BF16),
        flops=2 * both.shape[0] * half * columns,
    )


def add_kernel(_, mine, received, *outs):
    hid = outs[0].shape[2]
    for i, out in enumerate(outs):
        cols = slice(i * hid, (i + 1) * hid)
        out[0] = (mine[:, cols].astype(F32) + received[:, cols].astype(F32)).astype(BF16)


def shards(tokens, cotangent, expert_ids, probs, gate_weight, up_weight, down_weight):
    peers = ("x", "z")
    owners = lax.axis_size("x") * lax.axis_size("z")
    parts = lax.axis_size("y")
    middle = parts // 2
    core, place = lax.axis_index("dp"), lax.axis_index("y")
    tok, model = tokens.shape
    choose = expert_ids.shape[1]
    width = model // parts
    chunks = width // LANES
    hid = gate_weight.shape[2]
    capacity = min(tok, (5 * tok * choose + 4 * owners - 1) // (4 * owners))
    rows = owners * capacity
    first = core == 0
    swap = shift("dp", 1)
    place = place.astype(jnp.int32)
    position = jnp.stack((place, core.astype(jnp.int32)))

    def block_of(distance):
        return lax.rem(place - distance + 2 * parts, parts)

    flat, table = pack(
        expert_ids.T, probs.T, tokens, cotangent, place[None], width, owners, capacity
    )
    flat, gate_own, up_own, down_own = lax.optimization_barrier(
        (flat, gate_weight[0], up_weight[0], down_weight[0])
    )
    flat = lax.all_to_all(
        flat.reshape(owners, -1, LANES), peers, split_axis=0, concat_axis=0, tiled=True
    )

    gate_other = lax.ppermute(gate_own, "dp", swap)
    up_other = lax.ppermute(up_own, "dp", swap)
    down_other = lax.ppermute(down_own, "dp", swap)

    low = jnp.where(first, gate_own, up_other)
    high = jnp.where(first, gate_other, up_own)
    turn = jnp.concatenate((low, high)).reshape(parts, width, hid)
    turned = [None] * parts
    for d in sorted(range(parts), key=lambda d: -min(d, parts - d)):
        piece = lax.dynamic_index_in_dim(turn, block_of(-d), 0, keepdims=False)
        turned[d] = lax.ppermute(piece, "y", shift("y", d)) if d else piece
    turned_other = lax.ppermute(jnp.concatenate(turned), "dp", swap)

    flat, turned, turned_other, gate_other, up_other, down_other = lax.optimization_barrier(
        (flat, turned, turned_other, gate_other, up_other, down_other)
    )

    flat = flat.reshape(-1, LANES)
    own = local_call(
        lambda *refs: unpack_kernel(capacity, *refs),
        "unpack",
        position,
        (flat,),
        jax.ShapeDtypeStruct((rows, 2 * width), BF16),
        [pltpu.VMEM(flat.shape, F32)],
    )
    blocks = {0: own}
    right = left = own
    for d in range(1, middle):
        right = lax.ppermute(right, "y", shift("y", 1))
        left = lax.ppermute(left, "y", shift("y", -1))
        blocks[d], blocks[parts - d] = right, left
    x_mid = lax.ppermute(right[:, :width], "y", shift("y", 1))
    dy_mid = lax.ppermute(left[:, width:], "y", shift("y", -1))

    most = [d for d in range(parts) if d != middle]
    begun, piece = local_call(
        lambda *refs: forward_most(parts, most, middle, *refs),
        "forward_most",
        position,
        (
            *[blocks[d] for d in most],
            gate_own,
            gate_other,
            up_own,
            up_other,
            down_own,
            down_other,
        ),
        (
            jax.ShapeDtypeStruct((rows, 3 * hid), F32),
            jax.ShapeDtypeStruct((width, 3 * hid), BF16),
        ),
        flops=2 * rows * model * 3 * hid,
    )
    pair = jax.ShapeDtypeStruct((rows, 2 * hid), BF16)
    d_ordered, d_both, hidden = local_call(
        forward_last,
        "forward_last",
        position,
        (x_mid, dy_mid, piece, begun),
        (pair, pair, jax.ShapeDtypeStruct((rows, hid), BF16)),
        flops=2 * rows * width * 3 * hid,
    )

    d_ring = {0: d_ordered}
    right = left = d_ordered
    for d in range(1, middle + 1):
        right = lax.ppermute(right, "y", shift("y", 1))
        d_ring[d] = right
        if d < middle:
            left = lax.ppermute(left, "y", shift("y", -1))
            d_ring[parts - d] = left
    stretch = -(-capacity * chunks // TILE) * TILE
    d_rows = local_call(
        lambda *refs: back_kernel(parts, capacity, *refs),
        "back",
        position,
        (*[d_ring[d] for d in range(parts)], *turned, turned_other),
        jax.ShapeDtypeStruct((owners * stretch, LANES), BF16),
        [pltpu.VMEM((owners * stretch, LANES), F32)],
        flops=4 * rows * width * parts * hid,
    )
    operands = ([blocks[d] for d in most], x_mid, dy_mid, d_both, hidden)
    d_rows, operands = lax.optimization_barrier((d_rows, operands))
    returned = lax.all_to_all(
        d_rows.reshape(owners, -1, LANES), peers, split_axis=0, concat_axis=0, tiled=True
    )
    d_tokens = local_call(
        lambda *refs: combine_kernel(capacity, *refs),
        "combine",
        position,
        (returned.reshape(-1, LANES), table),
        jax.ShapeDtypeStruct((tok, width), BF16),
        [pltpu.VMEM((owners * stretch, LANES), F32), pltpu.VMEM((rows, width), BF16)],
        flops=1 << 37,
    )
    received = lax.ppermute(grads(place, 1 - core, *operands), "dp", swap)
    mine = grads(place, core, *operands)
    grad = jax.ShapeDtypeStruct(gate_weight.shape, BF16)
    return d_tokens, *local_call(
        add_kernel, "add", position, (mine, received), (grad, grad, grad)
    )


def solution(mesh):
    dp, experts, etp = mesh.devices.shape
    inner = min(16, experts)
    grid = Mesh(mesh.devices.reshape(dp, experts // inner, inner, etp), ("dp", "x", "z", "y"))
    row = P(("dp", "x", "z"), None)
    weight = P(("x", "z"), "dp", "y")
    return jax.shard_map(
        shards,
        mesh=grid,
        in_specs=(row, row, row, row, weight, weight, weight),
        out_specs=(P(("dp", "x", "z"), "y"), weight, weight, weight),
        check_vma=False,
    )
```

```python
import jax
import jax.numpy as jnp
from jax import lax
from jax.experimental import pallas as pl
from jax.experimental.pallas import tpu as pltpu
from jax.sharding import Mesh
from jax.sharding import PartitionSpec as P

F32 = jnp.float32
BF16 = jnp.bfloat16
LANES = 128
TILE = 8


def whole(shape):
    return pl.BlockSpec(
        shape, lambda *_: (0,) * len(shape), pipeline_mode=pl.Buffered(buffer_count=1)
    )


def local_call(kernel, name, scalars, operands, outs, scratch=(), flops=0, vmem=24):
    out_specs = jax.tree.map(lambda o: whole(o.shape), outs)
    return pl.pallas_call(
        kernel,
        grid=(1,),
        in_specs=[pl.BlockSpec(memory_space=pltpu.SMEM)] + [whole(o.shape) for o in operands],
        out_specs=out_specs,
        out_shape=outs,
        scratch_shapes=list(scratch),
        cost_estimate=pl.CostEstimate(flops=flops, bytes_accessed=1 << 20, transcendentals=0),
        compiler_params=pltpu.CompilerParams(vmem_limit_bytes=vmem << 20),
        name=name,
    )(scalars, *operands)


def transposed_dot(left, right):
    return lax.dot_general(left, right, (((0,), (0,)), ((), ())), preferred_element_type=F32)


def shift(axis, step):
    n = lax.axis_size(axis)
    return [(i, (i + step) % n) for i in range(n)]


def pack_kernel(capacity, col, ids_ref, probs_ref, x_ref, dy_ref, out_ref, table_ref, flat):
    choose, tok = ids_ref.shape
    rows = table_ref.shape[0]
    experts = rows // capacity
    chunks = x_ref.shape[1] // LANES
    stretch = flat.shape[0] // experts
    expert = lax.broadcasted_iota(jnp.int32, (experts, tok), 0)
    named = [expert == ids_ref[k : k + 1, :] for k in range(choose)]
    counts = sum(m.astype(F32) for m in named)
    earlier = lax.broadcasted_iota(jnp.int32, (tok, tok), 0) < lax.broadcasted_iota(
        jnp.int32, (tok, tok), 1
    )
    before = jnp.dot(
        counts.astype(BF16), earlier.astype(F32).astype(BF16), preferred_element_type=F32
    )
    row = lax.broadcasted_iota(jnp.int32, (rows, tok), 0)
    occupied = jnp.zeros((rows, tok), F32)
    weights = jnp.zeros((rows, tok), F32)
    for k in range(choose):
        slot = jnp.sum(jnp.where(named[k], before, 0.0), axis=0, keepdims=True)
        here = row == slot.astype(jnp.int32) * experts + ids_ref[k : k + 1, :]
        occupied = jnp.where(here, 1.0, occupied)
        weights = jnp.where(here, probs_ref[k : k + 1, :].astype(F32), weights)
    table = weights.astype(BF16)
    table_ref[...] = table
    placed = jnp.dot(occupied.astype(BF16), x_ref[...], preferred_element_type=F32)
    scaled = jnp.dot(table, dy_ref[...], preferred_element_type=F32)
    for s in range(capacity):
        of = slice(s * experts, (s + 1) * experts)
        for c in range(chunks):
            cols = slice(c * LANES, (c + 1) * LANES)
            at = s * 2 * chunks + c
            flat[pl.ds(at, experts, stride=stretch), :] = placed[of, cols]
            flat[pl.ds(at + chunks, experts, stride=stretch), :] = scaled[of, cols]
    out_ref[...] = flat[...].astype(BF16)


def pack(ids, probs, tokens, cotangent, column, width, experts, capacity):
    tok = tokens.shape[0]
    rows = experts * capacity
    height = rows * 2 * (width // LANES)
    wide = pl.BlockSpec((tok, width), lambda i, col: (0, col[0]))
    return pl.pallas_call(
        lambda *refs: pack_kernel(capacity, *refs),
        grid_spec=pltpu.PrefetchScalarGridSpec(
            num_scalar_prefetch=1,
            grid=(1,),
            in_specs=[whole(ids.shape), whole(probs.shape), wide, wide],
            out_specs=[whole((height, LANES)), whole((rows, tok))],
            scratch_shapes=[pltpu.VMEM((height, LANES), F32)],
        ),
        out_shape=[
            jax.ShapeDtypeStruct((height, LANES), BF16),
            jax.ShapeDtypeStruct((rows, tok), BF16),
        ],
        compiler_params=pltpu.CompilerParams(vmem_limit_bytes=60 << 20),
        name="pack",
    )(column, ids, probs, tokens, cotangent)


def unpack_kernel(capacity, _, flat_ref, x_ref, dy_ref, flat):
    rows, width = x_ref.shape
    owners, chunks = rows // capacity, width // LANES
    stretch = flat.shape[0] // owners
    flat[...] = flat_ref[...].astype(F32)
    for s in range(capacity):
        of = slice(s * owners, (s + 1) * owners)
        for c in range(chunks):
            cols = slice(c * LANES, (c + 1) * LANES)
            at = s * 2 * chunks + c
            x_ref[of, cols] = flat[pl.ds(at, owners, stride=stretch), :].astype(BF16)
            dy_ref[of, cols] = flat[pl.ds(at + chunks, owners, stride=stretch), :].astype(BF16)


def weights_at(parts, distance, position, width, weights):
    per_half = parts // 2
    source = lax.rem(position[0] - distance + parts, parts)
    of = pl.ds(pl.multiple_of(lax.rem(source, per_half) * width, width), width)
    half = source // per_half
    return jnp.concatenate([weights[half, i, of, :] for i in range(3)], axis=1)


def forward_most(parts, distances, middle, position, *refs):
    xs, dys = refs[: len(distances)], refs[len(distances) : 2 * len(distances)]
    weights, out, mid_ref = refs[2 * len(distances) :]
    rows, width = xs[0].shape
    hid = out.shape[1] // 3
    acc, back = jnp.zeros((rows, 2 * hid), F32), jnp.zeros((rows, hid), F32)
    for d, x, dy in zip(distances, xs, dys):
        piece = weights_at(parts, d, position, width, weights)
        acc = acc + jnp.dot(x[...], piece[:, : 2 * hid], preferred_element_type=F32)
        back = back + jnp.dot(dy[...], piece[:, 2 * hid :], preferred_element_type=F32)
    out[:, : 2 * hid] = acc
    out[:, 2 * hid :] = back
    mid_ref[...] = weights_at(parts, middle, position, width, weights)


def forward_last(_, x_ref, dy_ref, piece_ref, begun, both_ref, hidden_ref):
    hid = hidden_ref.shape[1]
    acc = begun[:, : 2 * hid] + jnp.dot(
        x_ref[...], piece_ref[:, : 2 * hid], preferred_element_type=F32
    )
    back = begun[:, 2 * hid :] + jnp.dot(
        dy_ref[...], piece_ref[:, 2 * hid :], preferred_element_type=F32
    )
    gate, up = acc[:, :hid], acc[:, hid:]
    sig = 1.0 / (1.0 + jnp.exp(-gate))
    act = gate * sig
    hidden_ref[...] = (act * up).astype(BF16)
    both_ref[:, :hid] = (back * up * sig * (1.0 + gate * (1.0 - sig))).astype(BF16)
    both_ref[:, hid:] = (back * act).astype(BF16)


def back_kernel(parts, capacity, position, *refs):
    blocks, (own_ref, other_ref, out_ref, flat) = refs[:parts], refs[parts:]
    place, core = position[0], position[1]
    per_half = parts // 2
    sub = own_ref.shape[0] // parts
    rows, width = blocks[0].shape[0], 2 * sub
    owners, chunks = rows // capacity, width // LANES
    stretch = flat.shape[0] // owners
    ahead = lax.rem(core + place // per_half, 2)
    own, other = jnp.zeros((rows, sub), F32), jnp.zeros((rows, sub), F32)
    contract = (((1,), (1,)), ((), ()))
    for d in range(parts):
        block = blocks[d][...]
        at = pl.multiple_of(lax.rem(d + per_half * ahead, parts) * sub, sub)
        own = own + lax.dot_general(
            block, own_ref[pl.ds(at, sub), :], contract, preferred_element_type=F32
        )
        at = pl.multiple_of(lax.rem(d + per_half * (1 - ahead), parts) * sub, sub)
        other = other + lax.dot_general(
            block, other_ref[pl.ds(at, sub), :], contract, preferred_element_type=F32
        )
    first = core == 0
    total = jnp.concatenate((jnp.where(first, own, other), jnp.where(first, other, own)), axis=1)
    for s in range(capacity):
        for c in range(chunks):
            flat[pl.ds(s * chunks + c, owners, stride=stretch), :] = total[
                s * owners : (s + 1) * owners, c * LANES : (c + 1) * LANES
            ]
    for pad in range(capacity * chunks, stretch):
        flat[pl.ds(pad, owners, stride=stretch), :] = jnp.zeros((owners, LANES), F32)
    out_ref[...] = flat[...].astype(BF16)


def combine_kernel(capacity, _, flat_ref, table_ref, out_ref, flat, rows_ref):
    rows, width = rows_ref.shape
    owners, chunks = rows // capacity, width // LANES
    stretch = flat.shape[0] // owners
    flat[...] = flat_ref[...].astype(F32)
    for s in range(capacity):
        for c in range(chunks):
            rows_ref[s * owners : (s + 1) * owners, c * LANES : (c + 1) * LANES] = flat[
                pl.ds(s * chunks + c, owners, stride=stretch), :
            ].astype(BF16)
    out_ref[...] = transposed_dot(table_ref[...], rows_ref[...]).astype(BF16)


def grads_kernel(parts, position, *refs):
    xs, dys, both_ref, hidden_ref = refs[:parts], refs[parts : 2 * parts], *refs[2 * parts :][:2]
    rest = refs[2 * parts + 2 :]
    place, wanted = position[0], position[1]
    width = xs[0].shape[1]
    hid = hidden_ref.shape[1]
    per_half = parts // 2
    for d in range(parts):
        source = lax.rem(place - d + parts, parts)

        @pl.when(source // per_half == wanted)
        def _():
            into = pl.ds(pl.multiple_of(lax.rem(source, per_half) * width, width), width)
            both = transposed_dot(xs[d][...], both_ref[...]).astype(BF16)
            down = transposed_dot(dys[d][...], hidden_ref[...]).astype(BF16)
            if len(rest) == 1:
                rest[0][into, : 2 * hid] = both
                rest[0][into, 2 * hid :] = down
            else:
                received, outs = rest[0], rest[1:]
                for i, share in enumerate((both[:, :hid], both[:, hid:], down)):
                    more = received[into, i * hid : (i + 1) * hid].astype(F32)
                    outs[i][0, into, :] = (share.astype(F32) + more).astype(BF16)


def grads(place, which, operands, outs):
    xs, dys, both, hidden, *received = operands
    parts = len(xs)
    half = parts // 2 * xs[0].shape[1]
    return local_call(
        lambda *refs: grads_kernel(parts, *refs),
        "grads",
        jnp.stack((place, which)).astype(jnp.int32),
        (*xs, *dys, both, hidden, *received),
        outs,
        flops=2 * both.shape[0] * half * (both.shape[1] + hidden.shape[1]),
    )


def shards(tokens, cotangent, expert_ids, probs, gate_weight, up_weight, down_weight):
    peers = ("x", "z")
    owners = lax.axis_size("x") * lax.axis_size("z")
    parts = lax.axis_size("y")
    core, place = lax.axis_index("dp"), lax.axis_index("y")
    tok, model = tokens.shape
    choose = expert_ids.shape[1]
    width = model // parts
    chunks = width // LANES
    hid = gate_weight.shape[2]
    capacity = min(tok, (5 * tok * choose + 4 * owners - 1) // (4 * owners))
    rows = owners * capacity
    half = parts // 2
    swap = shift("dp", 1)
    place, core = place.astype(jnp.int32), core.astype(jnp.int32)
    position = jnp.stack((place, core))

    flat, table = pack(
        expert_ids.T, probs.T, tokens, cotangent, place[None], width, owners, capacity
    )
    flat, own_weights = lax.optimization_barrier(
        (flat, (gate_weight[0], up_weight[0], down_weight[0]))
    )
    flat = lax.all_to_all(
        flat.reshape(owners, -1, LANES), peers, split_axis=0, concat_axis=0, tiled=True
    )
    weights = lax.all_gather(jnp.stack(own_weights), "dp")

    sub = width // 2
    turned = []
    for k in range(parts):
        target = lax.rem(place + k, parts)
        start = lax.rem(target, half) * width + target // half * sub
        piece = jnp.concatenate(
            [lax.dynamic_slice_in_dim(w, start, sub, 0) for w in own_weights[:2]], axis=1
        )
        perm = []
        for h in range(2):
            for p in range(parts):
                t = (p + k) % parts
                perm.append((h * parts + p, t // half * parts + h * half + t % half))
        turned.append(lax.ppermute(piece, ("dp", "y"), perm))
    flat, turned = lax.optimization_barrier((flat, turned))
    turned = jnp.concatenate(turned)
    turned_other = lax.ppermute(turned, "dp", swap)

    flat = flat.reshape(-1, LANES)
    pair = jax.ShapeDtypeStruct((rows, width), BF16)
    own = local_call(
        lambda *refs: unpack_kernel(capacity, *refs),
        "unpack",
        position,
        (flat,),
        (pair, pair),
        [pltpu.VMEM(flat.shape, F32)],
    )

    def ring(value, rightward):
        held = {0: value}
        right = left = value
        for d in range(1, half + 1):
            if d < half or rightward:
                right = lax.ppermute(right, "y", shift("y", 1))
                held[d] = right
            if d < half or not rightward:
                left = lax.ppermute(left, "y", shift("y", -1))
                held[parts - d] = left
        return [held[d] for d in range(parts)]

    xs, dys = ring(own[0], True), ring(own[1], False)
    most = [d for d in range(parts) if d != half]
    begun, piece = local_call(
        lambda *refs: forward_most(parts, most, half, *refs),
        "forward_most",
        position,
        (*[xs[d] for d in most], *[dys[d] for d in most], weights),
        (
            jax.ShapeDtypeStruct((rows, 3 * hid), F32),
            jax.ShapeDtypeStruct((width, 3 * hid), BF16),
        ),
        flops=2 * rows * model * 3 * hid,
    )
    d_both, hidden = local_call(
        forward_last,
        "forward_last",
        position,
        (xs[half], dys[half], piece, begun),
        (
            jax.ShapeDtypeStruct((rows, 2 * hid), BF16),
            jax.ShapeDtypeStruct((rows, hid), BF16),
        ),
        flops=2 * rows * width * 3 * hid,
    )

    stretch = -(-capacity * chunks // TILE) * TILE
    d_rows = local_call(
        lambda *refs: back_kernel(parts, capacity, *refs),
        "back",
        position,
        (*ring(d_both, True), turned, turned_other),
        jax.ShapeDtypeStruct((owners * stretch, LANES), BF16),
        [pltpu.VMEM((owners * stretch, LANES), F32)],
        flops=4 * rows * width * parts * hid,
    )
    d_rows, operands = lax.optimization_barrier((d_rows, (xs, dys, d_both, hidden)))
    returned = lax.all_to_all(
        d_rows.reshape(owners, -1, LANES), peers, split_axis=0, concat_axis=0, tiled=True
    )
    d_tokens = local_call(
        lambda *refs: combine_kernel(capacity, *refs),
        "combine",
        position,
        (returned.reshape(-1, LANES), table),
        jax.ShapeDtypeStruct((tok, width), BF16),
        [pltpu.VMEM((owners * stretch, LANES), F32), pltpu.VMEM((rows, width), BF16)],
        flops=1 << 37,
    )
    send = jax.ShapeDtypeStruct((model // 2, 3 * hid), BF16)
    received = lax.ppermute(grads(place, 1 - core, operands, send), "dp", swap)
    grad = jax.ShapeDtypeStruct(gate_weight.shape, BF16)
    return d_tokens, *grads(place, core, (*operands, received), (grad, grad, grad))


def solution(mesh):
    dp, experts, etp = mesh.devices.shape
    inner = min(16, experts)
    grid = Mesh(mesh.devices.reshape(dp, experts // inner, inner, etp), ("dp", "x", "z", "y"))
    row = P(("dp", "x", "z"), None)
    weight = P(("x", "z"), "dp", "y")
    return jax.shard_map(
        shards,
        mesh=grid,
        in_specs=(row, row, row, row, weight, weight, weight),
        out_specs=(P(("dp", "x", "z"), "y"), weight, weight, weight),
        check_vma=False,
    )
```

```python
import jax
import jax.numpy as jnp
from jax import lax
from jax.experimental import pallas as pl
from jax.experimental.pallas import tpu as pltpu
from jax.sharding import Mesh
from jax.sharding import PartitionSpec as P

F32 = jnp.float32
BF16 = jnp.bfloat16
LANES = 128
TILE = 8


def whole(shape):
    return pl.BlockSpec(
        shape, lambda *_: (0,) * len(shape), pipeline_mode=pl.Buffered(buffer_count=1)
    )


HBM = pl.BlockSpec(memory_space=pltpu.HBM)


def local_call(kernel, name, scalars, operands, outs, scratch=(), flops=0, far=(), vmem=24):
    out_specs = jax.tree.map(lambda o: whole(o.shape), outs)
    return pl.pallas_call(
        kernel,
        grid=(1,),
        in_specs=[pl.BlockSpec(memory_space=pltpu.SMEM)]
        + [whole(o.shape) for o in operands]
        + [HBM] * len(far),
        out_specs=out_specs,
        out_shape=outs,
        scratch_shapes=list(scratch),
        cost_estimate=pl.CostEstimate(flops=flops, bytes_accessed=1 << 20, transcendentals=0),
        compiler_params=pltpu.CompilerParams(vmem_limit_bytes=vmem << 20),
        name=name,
    )(scalars, *operands, *far)


def transposed_dot(left, right):
    return lax.dot_general(left, right, (((0,), (0,)), ((), ())), preferred_element_type=F32)


def shift(axis, step):
    n = lax.axis_size(axis)
    return [(i, (i + step) % n) for i in range(n)]


def pack_kernel(capacity, col, ids_ref, probs_ref, x_ref, dy_ref, out_ref, table_ref, flat):
    choose, tok = ids_ref.shape
    rows = table_ref.shape[0]
    experts = rows // capacity
    chunks = x_ref.shape[1] // LANES
    stretch = flat.shape[0] // experts
    expert = lax.broadcasted_iota(jnp.int32, (experts, tok), 0)
    named = [expert == ids_ref[k : k + 1, :] for k in range(choose)]
    counts = sum(m.astype(F32) for m in named)
    earlier = lax.broadcasted_iota(jnp.int32, (tok, tok), 0) < lax.broadcasted_iota(
        jnp.int32, (tok, tok), 1
    )
    before = jnp.dot(
        counts.astype(BF16), earlier.astype(F32).astype(BF16), preferred_element_type=F32
    )
    row = lax.broadcasted_iota(jnp.int32, (rows, tok), 0)
    occupied = jnp.zeros((rows, tok), F32)
    weights = jnp.zeros((rows, tok), F32)
    for k in range(choose):
        slot = jnp.sum(jnp.where(named[k], before, 0.0), axis=0, keepdims=True)
        here = row == slot.astype(jnp.int32) * experts + ids_ref[k : k + 1, :]
        occupied = jnp.where(here, 1.0, occupied)
        weights = jnp.where(here, probs_ref[k : k + 1, :].astype(F32), weights)
    table = weights.astype(BF16)
    table_ref[...] = table
    placed = jnp.dot(occupied.astype(BF16), x_ref[...], preferred_element_type=F32)
    scaled = jnp.dot(table, dy_ref[...], preferred_element_type=F32)
    for s in range(capacity):
        of = slice(s * experts, (s + 1) * experts)
        for c in range(chunks):
            cols = slice(c * LANES, (c + 1) * LANES)
            at = s * 2 * chunks + c
            flat[pl.ds(at, experts, stride=stretch), :] = placed[of, cols]
            flat[pl.ds(at + chunks, experts, stride=stretch), :] = scaled[of, cols]
    out_ref[...] = flat[...].astype(BF16)


def pack(ids, probs, tokens, cotangent, column, width, experts, capacity):
    tok = tokens.shape[0]
    rows = experts * capacity
    height = rows * 2 * (width // LANES)
    wide = pl.BlockSpec((tok, width), lambda i, col: (0, col[0]))
    return pl.pallas_call(
        lambda *refs: pack_kernel(capacity, *refs),
        grid_spec=pltpu.PrefetchScalarGridSpec(
            num_scalar_prefetch=1,
            grid=(1,),
            in_specs=[whole(ids.shape), whole(probs.shape), wide, wide],
            out_specs=[whole((height, LANES)), whole((rows, tok))],
            scratch_shapes=[pltpu.VMEM((height, LANES), F32)],
        ),
        out_shape=[
            jax.ShapeDtypeStruct((height, LANES), BF16),
            jax.ShapeDtypeStruct((rows, tok), BF16),
        ],
        compiler_params=pltpu.CompilerParams(vmem_limit_bytes=60 << 20),
        name="pack",
    )(column, ids, probs, tokens, cotangent)


def unpack_kernel(capacity, _, flat_ref, x_ref, dy_ref, flat):
    rows, width = x_ref.shape
    owners, chunks = rows // capacity, width // LANES
    stretch = flat.shape[0] // owners
    flat[...] = flat_ref[...].astype(F32)
    for s in range(capacity):
        of = slice(s * owners, (s + 1) * owners)
        for c in range(chunks):
            cols = slice(c * LANES, (c + 1) * LANES)
            at = s * 2 * chunks + c
            x_ref[of, cols] = flat[pl.ds(at, owners, stride=stretch), :].astype(BF16)
            dy_ref[of, cols] = flat[pl.ds(at + chunks, owners, stride=stretch), :].astype(BF16)


def bundle_kernel(_, *refs):
    pieces, weights, out = refs[:-4], refs[-4:-1], refs[-1]
    sub, wide = pieces[0].shape
    hid = weights[0].shape[1]
    for i, piece in enumerate(pieces):
        out[i * sub : (i + 1) * sub, :wide] = piece[...]
    for i, weight in enumerate(weights):
        out[:, wide + i * hid : wide + (i + 1) * hid] = weight[...]


def fetch(bundles, columns, held, sems):
    copies = [
        pltpu.make_async_copy(bundle.at[:, columns], held.at[i], sems.at[i])
        for i, bundle in enumerate(bundles)
    ]
    for copy in copies:
        copy.start()
    for copy in copies:
        copy.wait()


def weights_at(parts, distance, position, width, held):
    per_half = parts // 2
    source = lax.rem(position[0] - distance + parts, parts)
    of = pl.ds(pl.multiple_of(lax.rem(source, per_half) * width, width), width)
    return held[jnp.where(source // per_half == position[1], 0, 1), of, :]


def forward_most(parts, distances, middle, position, *refs):
    xs, dys = refs[: len(distances)], refs[len(distances) : 2 * len(distances)]
    own_bundle, other_bundle, out, mid_ref, held, sems = refs[2 * len(distances) :]
    rows, width = xs[0].shape
    hid = out.shape[1] // 3
    fetch((own_bundle, other_bundle), pl.ds(2 * hid, 3 * hid), held, sems)
    acc, back = jnp.zeros((rows, 2 * hid), F32), jnp.zeros((rows, hid), F32)
    for d, x, dy in zip(distances, xs, dys):
        piece = weights_at(parts, d, position, width, held)
        acc = acc + jnp.dot(x[...], piece[:, : 2 * hid], preferred_element_type=F32)
        back = back + jnp.dot(dy[...], piece[:, 2 * hid :], preferred_element_type=F32)
    out[:, : 2 * hid] = acc
    out[:, 2 * hid :] = back
    mid_ref[...] = weights_at(parts, middle, position, width, held)


def forward_last(_, x_ref, dy_ref, piece_ref, begun, both_ref, hidden_ref):
    hid = hidden_ref.shape[1]
    acc = begun[:, : 2 * hid] + jnp.dot(
        x_ref[...], piece_ref[:, : 2 * hid], preferred_element_type=F32
    )
    back = begun[:, 2 * hid :] + jnp.dot(
        dy_ref[...], piece_ref[:, 2 * hid :], preferred_element_type=F32
    )
    gate, up = acc[:, :hid], acc[:, hid:]
    sig = 1.0 / (1.0 + jnp.exp(-gate))
    act = gate * sig
    hidden_ref[...] = (act * up).astype(BF16)
    both_ref[:, :hid] = (back * up * sig * (1.0 + gate * (1.0 - sig))).astype(BF16)
    both_ref[:, hid:] = (back * act).astype(BF16)


def back_kernel(parts, capacity, position, *refs):
    blocks, (own_bundle, other_bundle, out_ref, flat, held, sems) = refs[:parts], refs[parts:]
    fetch((own_bundle, other_bundle), pl.ds(0, held.shape[2]), held, sems)
    place, core = position[0], position[1]
    per_half = parts // 2
    sub = held.shape[1] // parts
    rows, width = blocks[0].shape[0], 2 * sub
    owners, chunks = rows // capacity, width // LANES
    stretch = flat.shape[0] // owners
    ahead = lax.rem(core + place // per_half, 2)
    own, other = jnp.zeros((rows, sub), F32), jnp.zeros((rows, sub), F32)
    contract = (((1,), (1,)), ((), ()))
    for d in range(parts):
        block = blocks[d][...]
        at = pl.multiple_of(lax.rem(d + per_half * ahead, parts) * sub, sub)
        own = own + lax.dot_general(
            block, held[0, pl.ds(at, sub), :], contract, preferred_element_type=F32
        )
        at = pl.multiple_of(lax.rem(d + per_half * (1 - ahead), parts) * sub, sub)
        other = other + lax.dot_general(
            block, held[1, pl.ds(at, sub), :], contract, preferred_element_type=F32
        )
    first = core == 0
    total = jnp.concatenate((jnp.where(first, own, other), jnp.where(first, other, own)), axis=1)
    for s in range(capacity):
        for c in range(chunks):
            flat[pl.ds(s * chunks + c, owners, stride=stretch), :] = total[
                s * owners : (s + 1) * owners, c * LANES : (c + 1) * LANES
            ]
    for pad in range(capacity * chunks, stretch):
        flat[pl.ds(pad, owners, stride=stretch), :] = jnp.zeros((owners, LANES), F32)
    out_ref[...] = flat[...].astype(BF16)


def combine_kernel(capacity, _, flat_ref, table_ref, out_ref, flat, rows_ref):
    rows, width = rows_ref.shape
    owners, chunks = rows // capacity, width // LANES
    stretch = flat.shape[0] // owners
    flat[...] = flat_ref[...].astype(F32)
    for s in range(capacity):
        for c in range(chunks):
            rows_ref[s * owners : (s + 1) * owners, c * LANES : (c + 1) * LANES] = flat[
                pl.ds(s * chunks + c, owners, stride=stretch), :
            ].astype(BF16)
    out_ref[...] = transposed_dot(table_ref[...], rows_ref[...]).astype(BF16)


def grads_kernel(parts, position, *refs):
    xs, dys, both_ref, hidden_ref = refs[:parts], refs[parts : 2 * parts], *refs[2 * parts :][:2]
    rest = refs[2 * parts + 2 :]
    place, wanted = position[0], position[1]
    width = xs[0].shape[1]
    hid = hidden_ref.shape[1]
    per_half = parts // 2
    for d in range(parts):
        source = lax.rem(place - d + parts, parts)

        @pl.when(source // per_half == wanted)
        def _():
            into = pl.ds(pl.multiple_of(lax.rem(source, per_half) * width, width), width)
            both = transposed_dot(xs[d][...], both_ref[...]).astype(BF16)
            down = transposed_dot(dys[d][...], hidden_ref[...]).astype(BF16)
            for i, share in enumerate((both[:, :hid], both[:, hid:], down)):
                if len(rest) > 3:
                    more = rest[i][0, into, :].astype(F32)
                    share = (share.astype(F32) + more).astype(BF16)
                rest[i - 3][0, into, :] = share


def grads(place, which, operands, outs):
    xs, dys, both, hidden, *received = operands
    parts = len(xs)
    half = parts // 2 * xs[0].shape[1]
    return local_call(
        lambda *refs: grads_kernel(parts, *refs),
        "grads",
        jnp.stack((place, which)).astype(jnp.int32),
        (*xs, *dys, both, hidden, *received),
        outs,
        flops=2 * both.shape[0] * half * (both.shape[1] + hidden.shape[1]),
    )


def shards(tokens, cotangent, expert_ids, probs, gate_weight, up_weight, down_weight):
    peers = ("x", "z")
    owners = lax.axis_size("x") * lax.axis_size("z")
    parts = lax.axis_size("y")
    core, place = lax.axis_index("dp"), lax.axis_index("y")
    tok, model = tokens.shape
    choose = expert_ids.shape[1]
    width = model // parts
    chunks = width // LANES
    hid = gate_weight.shape[2]
    capacity = min(tok, (5 * tok * choose + 4 * owners - 1) // (4 * owners))
    rows = owners * capacity
    half = parts // 2
    swap = shift("dp", 1)
    place, core = place.astype(jnp.int32), core.astype(jnp.int32)
    position = jnp.stack((place, core))

    flat, table = pack(
        expert_ids.T, probs.T, tokens, cotangent, place[None], width, owners, capacity
    )
    flat, own_weights = lax.optimization_barrier(
        (flat, (gate_weight[0], up_weight[0], down_weight[0]))
    )
    flat = lax.all_to_all(
        flat.reshape(owners, -1, LANES), peers, split_axis=0, concat_axis=0, tiled=True
    )
    sub = width // 2
    turned = []
    for k in range(parts):
        target = lax.rem(place + k, parts)
        start = lax.rem(target, half) * width + target // half * sub
        piece = jnp.concatenate(
            [lax.dynamic_slice_in_dim(w, start, sub, 0) for w in own_weights[:2]], axis=1
        )
        perm = []
        for h in range(2):
            for p in range(parts):
                t = (p + k) % parts
                perm.append((h * parts + p, t // half * parts + h * half + t % half))
        turned.append(lax.ppermute(piece, ("dp", "y"), perm))
    flat, turned = lax.optimization_barrier((flat, turned))
    bundle = local_call(
        bundle_kernel,
        "bundle",
        position,
        (*turned, *own_weights),
        jax.ShapeDtypeStruct((model // 2, 5 * hid), BF16),
    )
    bundles = (bundle, lax.ppermute(bundle, "dp", swap))

    flat = flat.reshape(-1, LANES)
    pair = jax.ShapeDtypeStruct((rows, width), BF16)
    own = local_call(
        lambda *refs: unpack_kernel(capacity, *refs),
        "unpack",
        position,
        (flat,),
        (pair, pair),
        [pltpu.VMEM(flat.shape, F32)],
    )

    def ring(value, rightward):
        held = {0: value}
        right = left = value
        for d in range(1, half + 1):
            if d < half or rightward:
                right = lax.ppermute(right, "y", shift("y", 1))
                held[d] = right
            if d < half or not rightward:
                left = lax.ppermute(left, "y", shift("y", -1))
                held[parts - d] = left
        return [held[d] for d in range(parts)]

    xs, dys = ring(own[0], True), ring(own[1], False)
    most = [d for d in range(parts) if d != half]
    begun, piece = local_call(
        lambda *refs: forward_most(parts, most, half, *refs),
        "forward_most",
        position,
        (*[xs[d] for d in most], *[dys[d] for d in most]),
        (
            jax.ShapeDtypeStruct((rows, 3 * hid), F32),
            jax.ShapeDtypeStruct((width, 3 * hid), BF16),
        ),
        [pltpu.VMEM((2, model // 2, 3 * hid), BF16), pltpu.SemaphoreType.DMA((2,))],
        flops=2 * rows * model * 3 * hid,
        far=bundles,
    )
    d_both, hidden = local_call(
        forward_last,
        "forward_last",
        position,
        (xs[half], dys[half], piece, begun),
        (
            jax.ShapeDtypeStruct((rows, 2 * hid), BF16),
            jax.ShapeDtypeStruct((rows, hid), BF16),
        ),
        flops=2 * rows * width * 3 * hid,
    )

    stretch = -(-capacity * chunks // TILE) * TILE
    d_rows = local_call(
        lambda *refs: back_kernel(parts, capacity, *refs),
        "back",
        position,
        ring(d_both, True),
        jax.ShapeDtypeStruct((owners * stretch, LANES), BF16),
        [
            pltpu.VMEM((owners * stretch, LANES), F32),
            pltpu.VMEM((2, model // 2, 2 * hid), BF16),
            pltpu.SemaphoreType.DMA((2,)),
        ],
        flops=4 * rows * width * parts * hid,
        far=bundles,
    )
    d_rows, operands = lax.optimization_barrier((d_rows, (xs, dys, d_both, hidden)))
    returned = lax.all_to_all(
        d_rows.reshape(owners, -1, LANES), peers, split_axis=0, concat_axis=0, tiled=True
    )
    outs = (jax.ShapeDtypeStruct(gate_weight.shape, BF16),) * 3
    received = [
        lax.ppermute(share, "dp", swap) for share in grads(place, 1 - core, operands, outs)
    ]
    final = grads(place, core, (*operands, *received), outs)
    returned, final = lax.optimization_barrier((returned, final))
    d_tokens = local_call(
        lambda *refs: combine_kernel(capacity, *refs),
        "combine",
        position,
        (returned.reshape(-1, LANES), table),
        jax.ShapeDtypeStruct((tok, width), BF16),
        [pltpu.VMEM((owners * stretch, LANES), F32), pltpu.VMEM((rows, width), BF16)],
        flops=1 << 37,
    )
    return d_tokens, *final


def solution(mesh):
    dp, experts, etp = mesh.devices.shape
    inner = min(16, experts)
    grid = Mesh(mesh.devices.reshape(dp, experts // inner, inner, etp), ("dp", "x", "z", "y"))
    row = P(("dp", "x", "z"), None)
    weight = P(("x", "z"), "dp", "y")
    return jax.shard_map(
        shards,
        mesh=grid,
        in_specs=(row, row, row, row, weight, weight, weight),
        out_specs=(P(("dp", "x", "z"), "y"), weight, weight, weight),
        check_vma=False,
    )
```

```python
import jax
import jax.numpy as jnp
from jax import lax
from jax.experimental import pallas as pl
from jax.experimental.pallas import tpu as pltpu
from jax.sharding import Mesh
from jax.sharding import PartitionSpec as P

F32 = jnp.float32
BF16 = jnp.bfloat16
LANES = 128
TILE = 8


def whole(shape):
    return pl.BlockSpec(
        shape, lambda *_: (0,) * len(shape), pipeline_mode=pl.Buffered(buffer_count=1)
    )


HBM = pl.BlockSpec(memory_space=pltpu.HBM)


def local_call(kernel, name, scalars, operands, outs, scratch=(), flops=0, far=(), vmem=24):
    out_specs = jax.tree.map(lambda o: whole(o.shape), outs)
    return pl.pallas_call(
        kernel,
        grid=(1,),
        in_specs=[pl.BlockSpec(memory_space=pltpu.SMEM)]
        + [whole(o.shape) for o in operands]
        + [HBM] * len(far),
        out_specs=out_specs,
        out_shape=outs,
        scratch_shapes=list(scratch),
        cost_estimate=pl.CostEstimate(flops=flops, bytes_accessed=1 << 20, transcendentals=0),
        compiler_params=pltpu.CompilerParams(vmem_limit_bytes=vmem << 20),
        name=name,
    )(scalars, *operands, *far)


def transposed_dot(left, right):
    return lax.dot_general(left, right, (((0,), (0,)), ((), ())), preferred_element_type=F32)


def around(parts, step):
    pairs = []
    for p in range(parts):
        pairs.append((p, (p + step) % parts))
        pairs.append((parts + p, parts + (p - step) % parts))
    return pairs


def source_of(parts, position, distance):
    return lax.rem(position[0] - position[2] * distance + 2 * parts, parts)


def pack_kernel(capacity, col, ids_ref, probs_ref, x_ref, dy_ref, out_ref, table_ref, flat):
    choose, tok = ids_ref.shape
    rows = table_ref.shape[0]
    experts = rows // capacity
    chunks = x_ref.shape[1] // LANES
    stretch = flat.shape[0] // experts
    expert = lax.broadcasted_iota(jnp.int32, (experts, tok), 0)
    named = [expert == ids_ref[k : k + 1, :] for k in range(choose)]
    counts = sum(m.astype(F32) for m in named)
    earlier = lax.broadcasted_iota(jnp.int32, (tok, tok), 0) < lax.broadcasted_iota(
        jnp.int32, (tok, tok), 1
    )
    before = jnp.dot(
        counts.astype(BF16), earlier.astype(F32).astype(BF16), preferred_element_type=F32
    )
    row = lax.broadcasted_iota(jnp.int32, (rows, tok), 0)
    occupied = jnp.zeros((rows, tok), F32)
    weights = jnp.zeros((rows, tok), F32)
    for k in range(choose):
        slot = jnp.sum(jnp.where(named[k], before, 0.0), axis=0, keepdims=True)
        here = row == slot.astype(jnp.int32) * experts + ids_ref[k : k + 1, :]
        occupied = jnp.where(here, 1.0, occupied)
        weights = jnp.where(here, probs_ref[k : k + 1, :].astype(F32), weights)
    table = weights.astype(BF16)
    table_ref[...] = table
    placed = jnp.dot(occupied.astype(BF16), x_ref[...], preferred_element_type=F32)
    scaled = jnp.dot(table, dy_ref[...], preferred_element_type=F32)
    for s in range(capacity):
        of = slice(s * experts, (s + 1) * experts)
        for c in range(chunks):
            cols = slice(c * LANES, (c + 1) * LANES)
            at = s * 2 * chunks + c
            flat[pl.ds(at, experts, stride=stretch), :] = placed[of, cols]
            flat[pl.ds(at + chunks, experts, stride=stretch), :] = scaled[of, cols]
    out_ref[...] = flat[...].astype(BF16)


def pack(ids, probs, tokens, cotangent, column, width, experts, capacity):
    tok = tokens.shape[0]
    rows = experts * capacity
    height = rows * 2 * (width // LANES)
    wide = pl.BlockSpec((tok, width), lambda i, col: (0, col[0]))
    return pl.pallas_call(
        lambda *refs: pack_kernel(capacity, *refs),
        grid_spec=pltpu.PrefetchScalarGridSpec(
            num_scalar_prefetch=1,
            grid=(1,),
            in_specs=[whole(ids.shape), whole(probs.shape), wide, wide],
            out_specs=[whole((height, LANES)), whole((rows, tok))],
            scratch_shapes=[pltpu.VMEM((height, LANES), F32)],
        ),
        out_shape=[
            jax.ShapeDtypeStruct((height, LANES), BF16),
            jax.ShapeDtypeStruct((rows, tok), BF16),
        ],
        compiler_params=pltpu.CompilerParams(vmem_limit_bytes=60 << 20),
        name="pack",
    )(column, ids, probs, tokens, cotangent)


def unpack_kernel(capacity, _, flat_ref, x_ref, dy_ref, flat):
    rows, width = x_ref.shape
    owners, chunks = rows // capacity, width // LANES
    stretch = flat.shape[0] // owners
    flat[...] = flat_ref[...].astype(F32)
    for s in range(capacity):
        of = slice(s * owners, (s + 1) * owners)
        for c in range(chunks):
            cols = slice(c * LANES, (c + 1) * LANES)
            at = s * 2 * chunks + c
            x_ref[of, cols] = flat[pl.ds(at, owners, stride=stretch), :].astype(BF16)
            dy_ref[of, cols] = flat[pl.ds(at + chunks, owners, stride=stretch), :].astype(BF16)


def bundle_kernel(_, *refs):
    pieces, weights, out = refs[:-4], refs[-4:-1], refs[-1]
    sub, wide = pieces[0].shape
    hid = weights[0].shape[1]
    for i, piece in enumerate(pieces):
        out[i * sub : (i + 1) * sub, :wide] = piece[...]
    for i, weight in enumerate(weights):
        out[:, wide + i * hid : wide + (i + 1) * hid] = weight[...]


def fetch(bundles, columns, held, sems):
    copies = [
        pltpu.make_async_copy(bundle.at[:, columns], held.at[i], sems.at[i])
        for i, bundle in enumerate(bundles)
    ]
    for copy in copies:
        copy.start()
    for copy in copies:
        copy.wait()


def weights_at(parts, distance, position, width, held):
    per_half = parts // 2
    source = source_of(parts, position, distance)
    of = pl.ds(pl.multiple_of(lax.rem(source, per_half) * width, width), width)
    return held[jnp.where(source // per_half == position[1], 0, 1), of, :]


def forward_most(parts, distances, middle, position, *refs):
    xs, dys = refs[: len(distances)], refs[len(distances) : 2 * len(distances)]
    own_bundle, other_bundle, out, mid_ref, held, sems = refs[2 * len(distances) :]
    rows, width = xs[0].shape
    hid = out.shape[1] // 3
    fetch((own_bundle, other_bundle), pl.ds(2 * hid, 3 * hid), held, sems)
    acc, back = jnp.zeros((rows, 2 * hid), F32), jnp.zeros((rows, hid), F32)
    for d, x, dy in zip(distances, xs, dys):
        piece = weights_at(parts, d, position, width, held)
        acc = acc + jnp.dot(x[...], piece[:, : 2 * hid], preferred_element_type=F32)
        back = back + jnp.dot(dy[...], piece[:, 2 * hid :], preferred_element_type=F32)
    out[:, : 2 * hid] = acc
    out[:, 2 * hid :] = back
    mid_ref[...] = weights_at(parts, middle, position, width, held)


def forward_last(_, x_ref, dy_ref, piece_ref, begun, both_ref, hidden_ref):
    hid = hidden_ref.shape[1]
    acc = begun[:, : 2 * hid] + jnp.dot(
        x_ref[...], piece_ref[:, : 2 * hid], preferred_element_type=F32
    )
    back = begun[:, 2 * hid :] + jnp.dot(
        dy_ref[...], piece_ref[:, 2 * hid :], preferred_element_type=F32
    )
    gate, up = acc[:, :hid], acc[:, hid:]
    sig = 1.0 / (1.0 + jnp.exp(-gate))
    act = gate * sig
    hidden_ref[...] = (act * up).astype(BF16)
    both_ref[:, :hid] = (back * up * sig * (1.0 + gate * (1.0 - sig))).astype(BF16)
    both_ref[:, hid:] = (back * act).astype(BF16)


def back_kernel(parts, capacity, position, *refs):
    blocks, (own_bundle, other_bundle, out_ref, flat, held, sems) = refs[:parts], refs[parts:]
    fetch((own_bundle, other_bundle), pl.ds(0, held.shape[2]), held, sems)
    place, core = position[0], position[1]
    per_half = parts // 2
    sub = held.shape[1] // parts
    rows, width = blocks[0].shape[0], 2 * sub
    owners, chunks = rows // capacity, width // LANES
    stretch = flat.shape[0] // owners
    ahead = lax.rem(core + place // per_half, 2)
    own, other = jnp.zeros((rows, sub), F32), jnp.zeros((rows, sub), F32)
    contract = (((1,), (1,)), ((), ()))
    for d in range(parts):
        block = blocks[d][...]
        at = pl.multiple_of(lax.rem(position[2] * d + parts + per_half * ahead, parts) * sub, sub)
        own = own + lax.dot_general(
            block, held[0, pl.ds(at, sub), :], contract, preferred_element_type=F32
        )
        at = pl.multiple_of(lax.rem(position[2] * d + parts + per_half * (1 - ahead), parts) * sub, sub)
        other = other + lax.dot_general(
            block, held[1, pl.ds(at, sub), :], contract, preferred_element_type=F32
        )
    first = core == 0
    total = jnp.concatenate((jnp.where(first, own, other), jnp.where(first, other, own)), axis=1)
    for s in range(capacity):
        for c in range(chunks):
            flat[pl.ds(s * chunks + c, owners, stride=stretch), :] = total[
                s * owners : (s + 1) * owners, c * LANES : (c + 1) * LANES
            ]
    for pad in range(capacity * chunks, stretch):
        flat[pl.ds(pad, owners, stride=stretch), :] = jnp.zeros((owners, LANES), F32)
    out_ref[...] = flat[...].astype(BF16)


def combine_kernel(capacity, _, flat_ref, table_far, out_ref, flat, rows_ref, table, sem):
    copy = pltpu.make_async_copy(table_far, table, sem)
    copy.start()
    rows, width = rows_ref.shape
    owners, chunks = rows // capacity, width // LANES
    stretch = flat.shape[0] // owners
    flat[...] = flat_ref[...].astype(F32)
    for s in range(capacity):
        for c in range(chunks):
            rows_ref[s * owners : (s + 1) * owners, c * LANES : (c + 1) * LANES] = flat[
                pl.ds(s * chunks + c, owners, stride=stretch), :
            ].astype(BF16)
    copy.wait()
    out_ref[...] = transposed_dot(table[...], rows_ref[...]).astype(BF16)


def grads_kernel(parts, position, *refs):
    xs, dys, both_ref, hidden_ref = refs[:parts], refs[parts : 2 * parts], *refs[2 * parts :][:2]
    rest = refs[2 * parts + 2 :]
    wanted = position[1]
    width = xs[0].shape[1]
    hid = hidden_ref.shape[1]
    per_half = parts // 2
    for d in range(parts):
        source = source_of(parts, position, d)

        @pl.when(source // per_half == wanted)
        def _():
            into = pl.ds(pl.multiple_of(lax.rem(source, per_half) * width, width), width)
            both = transposed_dot(xs[d][...], both_ref[...]).astype(BF16)
            down = transposed_dot(dys[d][...], hidden_ref[...]).astype(BF16)
            for i, share in enumerate((both[:, :hid], both[:, hid:], down)):
                if len(rest) > 3:
                    more = rest[i][0, into, :].astype(F32)
                    share = (share.astype(F32) + more).astype(BF16)
                rest[i - 3][0, into, :] = share


def grads(position, which, operands, outs):
    xs, dys, both, hidden, *received = operands
    parts = len(xs)
    half = parts // 2 * xs[0].shape[1]
    return local_call(
        lambda *refs: grads_kernel(parts, *refs),
        "grads",
        position.at[1].set(which),
        (*xs, *dys, both, hidden, *received),
        outs,
        flops=2 * both.shape[0] * half * (both.shape[1] + hidden.shape[1]),
    )


def shards(tokens, cotangent, expert_ids, probs, gate_weight, up_weight, down_weight):
    peers = ("x", "z")
    owners = lax.axis_size("x") * lax.axis_size("z")
    parts = lax.axis_size("y")
    core, place = lax.axis_index("dp"), lax.axis_index("y")
    tok, model = tokens.shape
    choose = expert_ids.shape[1]
    width = model // parts
    chunks = width // LANES
    hid = gate_weight.shape[2]
    capacity = min(tok, (5 * tok * choose + 4 * owners - 1) // (4 * owners))
    rows = owners * capacity
    half = parts // 2
    swap = [(0, 1), (1, 0)]
    place, core = place.astype(jnp.int32), core.astype(jnp.int32)
    position = jnp.stack((place, core, 1 - 2 * core))

    flat, table = pack(
        expert_ids.T, probs.T, tokens, cotangent, place[None], width, owners, capacity
    )
    flat, own_weights = lax.optimization_barrier(
        (flat, (gate_weight[0], up_weight[0], down_weight[0]))
    )
    flat = lax.all_to_all(
        flat.reshape(owners, -1, LANES), peers, split_axis=0, concat_axis=0, tiled=True
    )
    sub = width // 2
    turned = []
    for k in range(parts):
        target = lax.rem(place + k, parts)
        start = lax.rem(target, half) * width + target // half * sub
        piece = jnp.concatenate(
            [lax.dynamic_slice_in_dim(w, start, sub, 0) for w in own_weights[:2]], axis=1
        )
        perm = []
        for h in range(2):
            for p in range(parts):
                t = (p + k) % parts
                perm.append((h * parts + p, t // half * parts + h * half + t % half))
        turned.append(lax.ppermute(piece, ("dp", "y"), perm))
    flat, turned = lax.optimization_barrier((flat, turned))
    bundle = local_call(
        bundle_kernel,
        "bundle",
        position,
        (*turned, *own_weights),
        jax.ShapeDtypeStruct((model // 2, 5 * hid), BF16),
    )
    bundles = (bundle, lax.ppermute(bundle, "dp", swap))
    flat = flat.reshape(-1, LANES)
    pair = jax.ShapeDtypeStruct((rows, width), BF16)
    own = local_call(
        lambda *refs: unpack_kernel(capacity, *refs),
        "unpack",
        position,
        (flat,),
        (pair, pair),
        [pltpu.VMEM(flat.shape, F32)],
    )

    def ring(value, rightward):
        held = {0: value}
        right = left = value
        for d in range(1, half + 1):
            if d < half or rightward:
                right = lax.ppermute(right, ("dp", "y"), around(parts, 1))
                held[d] = right
            if d < half or not rightward:
                left = lax.ppermute(left, ("dp", "y"), around(parts, -1))
                held[parts - d] = left
        return [held[d] for d in range(parts)]

    xs, dys = ring(own[0], True), ring(own[1], False)
    most = [d for d in range(parts) if d != half]
    begun, piece = local_call(
        lambda *refs: forward_most(parts, most, half, *refs),
        "forward_most",
        position,
        (*[xs[d] for d in most], *[dys[d] for d in most]),
        (
            jax.ShapeDtypeStruct((rows, 3 * hid), F32),
            jax.ShapeDtypeStruct((width, 3 * hid), BF16),
        ),
        [pltpu.VMEM((2, model // 2, 3 * hid), BF16), pltpu.SemaphoreType.DMA((2,))],
        flops=2 * rows * model * 3 * hid,
        far=bundles,
    )
    d_both, hidden = local_call(
        forward_last,
        "forward_last",
        position,
        (xs[half], dys[half], piece, begun),
        (
            jax.ShapeDtypeStruct((rows, 2 * hid), BF16),
            jax.ShapeDtypeStruct((rows, hid), BF16),
        ),
        flops=2 * rows * width * 3 * hid,
    )

    stretch = -(-capacity * chunks // TILE) * TILE
    d_rows = local_call(
        lambda *refs: back_kernel(parts, capacity, *refs),
        "back",
        position,
        ring(d_both, True),
        jax.ShapeDtypeStruct((owners * stretch, LANES), BF16),
        [
            pltpu.VMEM((owners * stretch, LANES), F32),
            pltpu.VMEM((2, model // 2, 2 * hid), BF16),
            pltpu.SemaphoreType.DMA((2,)),
        ],
        flops=4 * rows * width * parts * hid,
        far=bundles,
    )
    d_rows, operands = lax.optimization_barrier((d_rows, (xs, dys, d_both, hidden)))
    returned = lax.all_to_all(
        d_rows.reshape(owners, -1, LANES), peers, split_axis=0, concat_axis=0, tiled=True
    )
    outs = (jax.ShapeDtypeStruct(gate_weight.shape, BF16),) * 3
    received = [
        lax.ppermute(share, "dp", swap) for share in grads(position, 1 - core, operands, outs)
    ]
    final = grads(position, core, (*operands, *received), outs)
    returned, final = lax.optimization_barrier((returned, final))
    d_tokens = local_call(
        lambda *refs: combine_kernel(capacity, *refs),
        "combine",
        position,
        (returned.reshape(-1, LANES),),
        jax.ShapeDtypeStruct((tok, width), BF16),
        [
            pltpu.VMEM((owners * stretch, LANES), F32),
            pltpu.VMEM((rows, width), BF16),
            pltpu.VMEM(table.shape, BF16),
            pltpu.SemaphoreType.DMA(()),
        ],
        far=(table,),
        vmem=60,
    )
    return d_tokens, *final


def solution(mesh):
    dp, experts, etp = mesh.devices.shape
    inner = min(16, experts)
    grid = Mesh(mesh.devices.reshape(dp, experts // inner, inner, etp), ("dp", "x", "z", "y"))
    row = P(("dp", "x", "z"), None)
    weight = P(("x", "z"), "dp", "y")
    return jax.shard_map(
        shards,
        mesh=grid,
        in_specs=(row, row, row, row, weight, weight, weight),
        out_specs=(P(("dp", "x", "z"), "y"), weight, weight, weight),
        check_vma=False,
    )
```

```python
import jax
import jax.numpy as jnp
from jax import lax
from jax.experimental import pallas as pl
from jax.experimental.pallas import tpu as pltpu
from jax.sharding import Mesh
from jax.sharding import PartitionSpec as P

F32 = jnp.float32
BF16 = jnp.bfloat16
LANES = 128
TILE = 8


def whole(shape):
    return pl.BlockSpec(
        shape, lambda *_: (0,) * len(shape), pipeline_mode=pl.Buffered(buffer_count=1)
    )


HBM = pl.BlockSpec(memory_space=pltpu.HBM)


def local_call(kernel, name, scalars, operands, outs, scratch=(), flops=0, far=(), vmem=24):
    out_specs = jax.tree.map(lambda o: whole(o.shape), outs)
    return pl.pallas_call(
        kernel,
        grid=(1,),
        in_specs=[pl.BlockSpec(memory_space=pltpu.SMEM)]
        + [whole(o.shape) for o in operands]
        + [HBM] * len(far),
        out_specs=out_specs,
        out_shape=outs,
        scratch_shapes=list(scratch),
        cost_estimate=pl.CostEstimate(flops=flops, bytes_accessed=1 << 20, transcendentals=0),
        compiler_params=pltpu.CompilerParams(vmem_limit_bytes=vmem << 20),
        name=name,
    )(scalars, *operands, *far)


def transposed_dot(left, right):
    return lax.dot_general(left, right, (((0,), (0,)), ((), ())), preferred_element_type=F32)


def shift(parts, step):
    return [(p, (p + step) % parts) for p in range(parts)]


def around(parts, step):
    pairs = []
    for p in range(parts):
        pairs.append((p, (p + step) % parts))
        pairs.append((parts + p, parts + (p - step) % parts))
    return pairs


def source_of(parts, position, distance):
    return lax.rem(position[0] - position[2] * distance + 2 * parts, parts)


def pack_kernel(capacity, col, ids_ref, probs_ref, x_ref, dy_ref, out_ref, table_ref, flat):
    choose, tok = ids_ref.shape
    rows = table_ref.shape[0]
    experts = rows // capacity
    chunks = x_ref.shape[1] // LANES
    stretch = flat.shape[0] // experts
    expert = lax.broadcasted_iota(jnp.int32, (experts, tok), 0)
    named = [expert == ids_ref[k : k + 1, :] for k in range(choose)]
    counts = sum(m.astype(F32) for m in named)
    earlier = lax.broadcasted_iota(jnp.int32, (tok, tok), 0) < lax.broadcasted_iota(
        jnp.int32, (tok, tok), 1
    )
    before = jnp.dot(
        counts.astype(BF16), earlier.astype(F32).astype(BF16), preferred_element_type=F32
    )
    row = lax.broadcasted_iota(jnp.int32, (rows, tok), 0)
    occupied = jnp.zeros((rows, tok), F32)
    weights = jnp.zeros((rows, tok), F32)
    for k in range(choose):
        slot = jnp.sum(jnp.where(named[k], before, 0.0), axis=0, keepdims=True)
        here = row == slot.astype(jnp.int32) * experts + ids_ref[k : k + 1, :]
        occupied = jnp.where(here, 1.0, occupied)
        weights = jnp.where(here, probs_ref[k : k + 1, :].astype(F32), weights)
    table = weights.astype(BF16)
    table_ref[...] = table
    placed = jnp.dot(occupied.astype(BF16), x_ref[...], preferred_element_type=F32)
    scaled = jnp.dot(table, dy_ref[...], preferred_element_type=F32)
    for s in range(capacity):
        of = slice(s * experts, (s + 1) * experts)
        for c in range(chunks):
            cols = slice(c * LANES, (c + 1) * LANES)
            at = s * 2 * chunks + c
            flat[pl.ds(at, experts, stride=stretch), :] = placed[of, cols]
            flat[pl.ds(at + chunks, experts, stride=stretch), :] = scaled[of, cols]
    out_ref[...] = flat[...].astype(BF16)


def pack(ids, probs, tokens, cotangent, column, width, experts, capacity):
    tok = tokens.shape[0]
    rows = experts * capacity
    height = rows * 2 * (width // LANES)
    wide = pl.BlockSpec((tok, width), lambda i, col: (0, col[0]))
    return pl.pallas_call(
        lambda *refs: pack_kernel(capacity, *refs),
        grid_spec=pltpu.PrefetchScalarGridSpec(
            num_scalar_prefetch=1,
            grid=(1,),
            in_specs=[whole(ids.shape), whole(probs.shape), wide, wide],
            out_specs=[whole((height, LANES)), whole((rows, tok))],
            scratch_shapes=[pltpu.VMEM((height, LANES), F32)],
        ),
        out_shape=[
            jax.ShapeDtypeStruct((height, LANES), BF16),
            jax.ShapeDtypeStruct((rows, tok), BF16),
        ],
        compiler_params=pltpu.CompilerParams(vmem_limit_bytes=60 << 20),
        name="pack",
    )(column, ids, probs, tokens, cotangent)


def unpack_kernel(capacity, _, flat_ref, out_ref, flat):
    rows, width = out_ref.shape
    owners, chunks = rows // capacity, width // LANES
    stretch = flat.shape[0] // owners
    flat[...] = flat_ref[...].astype(F32)
    for s in range(capacity):
        for c in range(chunks):
            out_ref[s * owners : (s + 1) * owners, c * LANES : (c + 1) * LANES] = flat[
                pl.ds(s * chunks + c, owners, stride=stretch), :
            ].astype(BF16)


def bundle_kernel(_, *refs):
    pieces, weights, out = refs[:-4], refs[-4:-1], refs[-1]
    sub, wide = pieces[0].shape
    hid = weights[0].shape[1]
    for i, piece in enumerate(pieces):
        out[i * sub : (i + 1) * sub, :wide] = piece[...]
    for i, weight in enumerate(weights):
        out[:, wide + i * hid : wide + (i + 1) * hid] = weight[...]


def fetch(bundles, columns, held, sems):
    copies = [
        pltpu.make_async_copy(bundle.at[:, columns], held.at[i], sems.at[i])
        for i, bundle in enumerate(bundles)
    ]
    for copy in copies:
        copy.start()
    for copy in copies:
        copy.wait()


def weights_at(parts, distance, position, width, held):
    per_half = parts // 2
    source = source_of(parts, position, distance)
    of = pl.ds(pl.multiple_of(lax.rem(source, per_half) * width, width), width)
    return held[jnp.where(source // per_half == position[1], 0, 1), of, :]


def forward_most(parts, distances, middle, position, *refs):
    blocks, (own_bundle, other_bundle, out, mid_ref, held, sems) = (
        refs[: len(distances)],
        refs[len(distances) :],
    )
    rows, width = blocks[0].shape[0], blocks[0].shape[1] // 2
    hid = out.shape[1] // 3
    fetch((own_bundle, other_bundle), pl.ds(2 * hid, 3 * hid), held, sems)
    acc, back = jnp.zeros((rows, 2 * hid), F32), jnp.zeros((rows, hid), F32)
    for d, block in zip(distances, blocks):
        piece = weights_at(parts, d, position, width, held)
        acc = acc + jnp.dot(block[:, :width], piece[:, : 2 * hid], preferred_element_type=F32)
        back = back + jnp.dot(block[:, width:], piece[:, 2 * hid :], preferred_element_type=F32)
    out[:, : 2 * hid] = acc
    out[:, 2 * hid :] = back
    mid_ref[...] = weights_at(parts, middle, position, width, held)


def forward_last(_, block, piece_ref, begun, both_ref, hidden_ref):
    hid, width = hidden_ref.shape[1], block.shape[1] // 2
    acc = begun[:, : 2 * hid] + jnp.dot(
        block[:, :width], piece_ref[:, : 2 * hid], preferred_element_type=F32
    )
    back = begun[:, 2 * hid :] + jnp.dot(
        block[:, width:], piece_ref[:, 2 * hid :], preferred_element_type=F32
    )
    gate, up = acc[:, :hid], acc[:, hid:]
    sig = 1.0 / (1.0 + jnp.exp(-gate))
    act = gate * sig
    hidden_ref[...] = (act * up).astype(BF16)
    both_ref[:, :hid] = (back * up * sig * (1.0 + gate * (1.0 - sig))).astype(BF16)
    both_ref[:, hid:] = (back * act).astype(BF16)


def back_kernel(parts, capacity, position, *refs):
    blocks, (own_bundle, other_bundle, out_ref, flat, held, sems) = refs[:parts], refs[parts:]
    fetch((own_bundle, other_bundle), pl.ds(0, held.shape[2]), held, sems)
    place, core = position[0], position[1]
    per_half = parts // 2
    sub = held.shape[1] // parts
    rows, width = blocks[0].shape[0], 2 * sub
    owners, chunks = rows // capacity, width // LANES
    stretch = flat.shape[0] // owners
    ahead = lax.rem(core + place // per_half, 2)
    own, other = jnp.zeros((rows, sub), F32), jnp.zeros((rows, sub), F32)
    contract = (((1,), (1,)), ((), ()))
    for d in range(parts):
        block = blocks[d][...]
        at = pl.multiple_of(lax.rem(position[2] * d + parts + per_half * ahead, parts) * sub, sub)
        own = own + lax.dot_general(
            block, held[0, pl.ds(at, sub), :], contract, preferred_element_type=F32
        )
        at = pl.multiple_of(lax.rem(position[2] * d + parts + per_half * (1 - ahead), parts) * sub, sub)
        other = other + lax.dot_general(
            block, held[1, pl.ds(at, sub), :], contract, preferred_element_type=F32
        )
    first = core == 0
    total = jnp.concatenate((jnp.where(first, own, other), jnp.where(first, other, own)), axis=1)
    for s in range(capacity):
        for c in range(chunks):
            flat[pl.ds(s * chunks + c, owners, stride=stretch), :] = total[
                s * owners : (s + 1) * owners, c * LANES : (c + 1) * LANES
            ]
    for pad in range(capacity * chunks, stretch):
        flat[pl.ds(pad, owners, stride=stretch), :] = jnp.zeros((owners, LANES), F32)
    out_ref[...] = flat[...].astype(BF16)


def combine_kernel(capacity, _, flat_ref, table_far, out_ref, flat, rows_ref, table, sem):
    copy = pltpu.make_async_copy(table_far, table, sem)
    copy.start()
    rows, width = rows_ref.shape
    owners, chunks = rows // capacity, width // LANES
    stretch = flat.shape[0] // owners
    flat[...] = flat_ref[...].astype(F32)
    for s in range(capacity):
        for c in range(chunks):
            rows_ref[s * owners : (s + 1) * owners, c * LANES : (c + 1) * LANES] = flat[
                pl.ds(s * chunks + c, owners, stride=stretch), :
            ].astype(BF16)
    copy.wait()
    out_ref[...] = transposed_dot(table[...], rows_ref[...]).astype(BF16)


def grads_kernel(parts, position, *refs):
    blocks, (both_ref, hidden_ref, *rest) = refs[:parts], refs[parts:]
    wanted = position[1]
    width = blocks[0].shape[1] // 2
    hid = hidden_ref.shape[1]
    per_half = parts // 2
    for d in range(parts):
        source = source_of(parts, position, d)

        @pl.when(source // per_half == wanted)
        def _():
            into = pl.ds(pl.multiple_of(lax.rem(source, per_half) * width, width), width)
            both = transposed_dot(blocks[d][:, :width], both_ref[...]).astype(BF16)
            down = transposed_dot(blocks[d][:, width:], hidden_ref[...]).astype(BF16)
            for i, share in enumerate((both[:, :hid], both[:, hid:], down)):
                if len(rest) > 3:
                    more = rest[i][0, into, :].astype(F32)
                    share = (share.astype(F32) + more).astype(BF16)
                rest[i - 3][0, into, :] = share


def grads(position, which, operands, outs):
    blocks, both, hidden, *received = operands
    parts = len(blocks)
    half = parts // 2 * (blocks[0].shape[1] // 2)
    return local_call(
        lambda *refs: grads_kernel(parts, *refs),
        "grads",
        position.at[1].set(which),
        (*blocks, both, hidden, *received),
        outs,
        flops=2 * both.shape[0] * half * (both.shape[1] + hidden.shape[1]),
    )


def shards(tokens, cotangent, expert_ids, probs, gate_weight, up_weight, down_weight):
    peers = ("x", "z")
    owners = lax.axis_size("x") * lax.axis_size("z")
    parts = lax.axis_size("y")
    core, place = lax.axis_index("dp"), lax.axis_index("y")
    tok, model = tokens.shape
    choose = expert_ids.shape[1]
    width = model // parts
    chunks = width // LANES
    hid = gate_weight.shape[2]
    capacity = min(tok, (5 * tok * choose + 4 * owners - 1) // (4 * owners))
    rows = owners * capacity
    half = parts // 2
    swap = [(0, 1), (1, 0)]
    place, core = place.astype(jnp.int32), core.astype(jnp.int32)
    position = jnp.stack((place, core, 1 - 2 * core))

    flat, table = pack(
        expert_ids.T, probs.T, tokens, cotangent, place[None], width, owners, capacity
    )
    flat, own_weights = lax.optimization_barrier(
        (flat, (gate_weight[0], up_weight[0], down_weight[0]))
    )
    flat = lax.all_to_all(
        flat.reshape(owners, -1, LANES), peers, split_axis=0, concat_axis=0, tiled=True
    )
    sub = width // 2
    turned = []
    for k in range(parts):
        target = lax.rem(place + k, parts)
        start = lax.rem(target, half) * width + target // half * sub
        piece = jnp.concatenate(
            [lax.dynamic_slice_in_dim(w, start, sub, 0) for w in own_weights[:2]], axis=1
        )
        perm = []
        for h in range(2):
            for p in range(parts):
                t = (p + k) % parts
                perm.append((h * parts + p, t // half * parts + h * half + t % half))
        turned.append(lax.ppermute(piece, ("dp", "y"), perm))
    flat, turned = lax.optimization_barrier((flat, turned))
    bundle = local_call(
        bundle_kernel,
        "bundle",
        position,
        (*turned, *own_weights),
        jax.ShapeDtypeStruct((model // 2, 5 * hid), BF16),
    )
    bundles = (bundle, lax.ppermute(bundle, "dp", swap))
    flat = flat.reshape(-1, LANES)
    own = local_call(
        lambda *refs: unpack_kernel(capacity, *refs),
        "unpack",
        position,
        (flat,),
        jax.ShapeDtypeStruct((rows, 2 * width), BF16),
        [pltpu.VMEM(flat.shape, F32)],
    )

    def ring(value, axes, on, back):
        held = {0: value}
        ahead = behind = value
        for d in range(1, half + 1):
            ahead = lax.ppermute(ahead, axes, on)
            held[d] = ahead
            if d < half:
                behind = lax.ppermute(behind, axes, back)
                held[parts - d] = behind
        return [held[d] for d in range(parts)]

    blocks = ring(own, ("dp", "y"), around(parts, 1), around(parts, -1))
    most = [d for d in range(parts) if d != half]
    begun, piece = local_call(
        lambda *refs: forward_most(parts, most, half, *refs),
        "forward_most",
        position,
        [blocks[d] for d in most],
        (
            jax.ShapeDtypeStruct((rows, 3 * hid), F32),
            jax.ShapeDtypeStruct((width, 3 * hid), BF16),
        ),
        [pltpu.VMEM((2, model // 2, 3 * hid), BF16), pltpu.SemaphoreType.DMA((2,))],
        flops=2 * rows * model * 3 * hid,
        far=bundles,
    )
    d_both, hidden = local_call(
        forward_last,
        "forward_last",
        position,
        (blocks[half], piece, begun),
        (
            jax.ShapeDtypeStruct((rows, 2 * hid), BF16),
            jax.ShapeDtypeStruct((rows, hid), BF16),
        ),
        flops=2 * rows * width * 3 * hid,
    )

    stretch = -(-capacity * chunks // TILE) * TILE
    d_rows = local_call(
        lambda *refs: back_kernel(parts, capacity, *refs),
        "back",
        position.at[2].set(1),
        ring(d_both, "y", shift(parts, 1), shift(parts, -1)),
        jax.ShapeDtypeStruct((owners * stretch, LANES), BF16),
        [
            pltpu.VMEM((owners * stretch, LANES), F32),
            pltpu.VMEM((2, model // 2, 2 * hid), BF16),
            pltpu.SemaphoreType.DMA((2,)),
        ],
        flops=4 * rows * width * parts * hid,
        far=bundles,
    )
    d_rows, operands = lax.optimization_barrier((d_rows, (blocks, d_both, hidden)))
    returned = lax.all_to_all(
        d_rows.reshape(owners, -1, LANES), peers, split_axis=0, concat_axis=0, tiled=True
    )
    outs = (jax.ShapeDtypeStruct(gate_weight.shape, BF16),) * 3
    received = [
        lax.ppermute(share, "dp", swap) for share in grads(position, 1 - core, operands, outs)
    ]
    final = grads(position, core, (*operands, *received), outs)
    returned, final = lax.optimization_barrier((returned, final))
    d_tokens = local_call(
        lambda *refs: combine_kernel(capacity, *refs),
        "combine",
        position,
        (returned.reshape(-1, LANES),),
        jax.ShapeDtypeStruct((tok, width), BF16),
        [
            pltpu.VMEM((owners * stretch, LANES), F32),
            pltpu.VMEM((rows, width), BF16),
            pltpu.VMEM(table.shape, BF16),
            pltpu.SemaphoreType.DMA(()),
        ],
        far=(table,),
        vmem=60,
    )
    return d_tokens, *final


def solution(mesh):
    dp, experts, etp = mesh.devices.shape
    inner = min(16, experts)
    grid = Mesh(mesh.devices.reshape(dp, experts // inner, inner, etp), ("dp", "x", "z", "y"))
    row = P(("dp", "x", "z"), None)
    weight = P(("x", "z"), "dp", "y")
    return jax.shard_map(
        shards,
        mesh=grid,
        in_specs=(row, row, row, row, weight, weight, weight),
        out_specs=(P(("dp", "x", "z"), "y"), weight, weight, weight),
        check_vma=False,
    )
```

```python
import jax
import jax.numpy as jnp
from jax import lax
from jax.experimental import pallas as pl
from jax.experimental.pallas import tpu as pltpu
from jax.sharding import Mesh
from jax.sharding import PartitionSpec as P

F32 = jnp.float32
BF16 = jnp.bfloat16
LANES = 128
TILE = 8


def whole(shape):
    return pl.BlockSpec(
        shape, lambda *_: (0,) * len(shape), pipeline_mode=pl.Buffered(buffer_count=1)
    )


HBM = pl.BlockSpec(memory_space=pltpu.HBM)


def local_call(kernel, name, scalars, operands, outs, scratch=(), flops=0, far=(), vmem=24):
    out_specs = jax.tree.map(lambda o: whole(o.shape), outs)
    return pl.pallas_call(
        kernel,
        grid=(1,),
        in_specs=[pl.BlockSpec(memory_space=pltpu.SMEM)]
        + [whole(o.shape) for o in operands]
        + [HBM] * len(far),
        out_specs=out_specs,
        out_shape=outs,
        scratch_shapes=list(scratch),
        cost_estimate=pl.CostEstimate(flops=flops, bytes_accessed=1 << 20, transcendentals=0),
        compiler_params=pltpu.CompilerParams(vmem_limit_bytes=vmem << 20),
        name=name,
    )(scalars, *operands, *far)


def transposed_dot(left, right):
    return lax.dot_general(left, right, (((0,), (0,)), ((), ())), preferred_element_type=F32)


def shift(parts, step):
    return [(p, (p + step) % parts) for p in range(parts)]


def around(parts, step):
    pairs = []
    for p in range(parts):
        pairs.append((p, (p + step) % parts))
        pairs.append((parts + p, parts + (p - step) % parts))
    return pairs


def source_of(parts, position, distance):
    return lax.rem(position[0] - position[2] * distance + 2 * parts, parts)


def pack_kernel(capacity, col, ids_ref, probs_ref, x_ref, dy_ref, out_ref, table_ref, flat):
    choose, tok = ids_ref.shape
    rows = table_ref.shape[0]
    experts = rows // capacity
    chunks = x_ref.shape[1] // LANES
    stretch = flat.shape[0] // experts
    expert = lax.broadcasted_iota(jnp.int32, (experts, tok), 0)
    named = [expert == ids_ref[k : k + 1, :] for k in range(choose)]
    counts = sum(m.astype(F32) for m in named)
    earlier = lax.broadcasted_iota(jnp.int32, (tok, tok), 0) < lax.broadcasted_iota(
        jnp.int32, (tok, tok), 1
    )
    before = jnp.dot(
        counts.astype(BF16), earlier.astype(F32).astype(BF16), preferred_element_type=F32
    )
    row = lax.broadcasted_iota(jnp.int32, (rows, tok), 0)
    occupied = jnp.zeros((rows, tok), F32)
    weights = jnp.zeros((rows, tok), F32)
    for k in range(choose):
        slot = jnp.sum(jnp.where(named[k], before, 0.0), axis=0, keepdims=True)
        here = row == slot.astype(jnp.int32) * experts + ids_ref[k : k + 1, :]
        occupied = jnp.where(here, 1.0, occupied)
        weights = jnp.where(here, probs_ref[k : k + 1, :].astype(F32), weights)
    table = weights.astype(BF16)
    table_ref[...] = table
    placed = jnp.dot(occupied.astype(BF16), x_ref[...], preferred_element_type=F32)
    scaled = jnp.dot(table, dy_ref[...], preferred_element_type=F32)
    for s in range(capacity):
        of = slice(s * experts, (s + 1) * experts)
        for c in range(chunks):
            cols = slice(c * LANES, (c + 1) * LANES)
            at = s * 2 * chunks + c
            flat[pl.ds(at, experts, stride=stretch), :] = placed[of, cols]
            flat[pl.ds(at + chunks, experts, stride=stretch), :] = scaled[of, cols]
    out_ref[...] = flat[...].astype(BF16)


def pack(ids, probs, tokens, cotangent, column, width, experts, capacity):
    tok = tokens.shape[0]
    rows = experts * capacity
    height = rows * 2 * (width // LANES)
    wide = pl.BlockSpec((tok, width), lambda i, col: (0, col[0]))
    return pl.pallas_call(
        lambda *refs: pack_kernel(capacity, *refs),
        grid_spec=pltpu.PrefetchScalarGridSpec(
            num_scalar_prefetch=1,
            grid=(1,),
            in_specs=[whole(ids.shape), whole(probs.shape), wide, wide],
            out_specs=[whole((height, LANES)), whole((rows, tok))],
            scratch_shapes=[pltpu.VMEM((height, LANES), F32)],
        ),
        out_shape=[
            jax.ShapeDtypeStruct((height, LANES), BF16),
            jax.ShapeDtypeStruct((rows, tok), BF16),
        ],
        compiler_params=pltpu.CompilerParams(vmem_limit_bytes=60 << 20),
        name="pack",
    )(column, ids, probs, tokens, cotangent)


def unpack_kernel(capacity, _, flat_ref, x_ref, dy_ref, flat):
    rows, width = x_ref.shape
    owners, chunks = rows // capacity, width // LANES
    stretch = flat.shape[0] // owners
    flat[...] = flat_ref[...].astype(F32)
    for s in range(capacity):
        of = slice(s * owners, (s + 1) * owners)
        for c in range(chunks):
            cols = slice(c * LANES, (c + 1) * LANES)
            at = s * 2 * chunks + c
            x_ref[of, cols] = flat[pl.ds(at, owners, stride=stretch), :].astype(BF16)
            dy_ref[of, cols] = flat[pl.ds(at + chunks, owners, stride=stretch), :].astype(BF16)


def bundle_kernel(_, *refs):
    pieces, weights, out = refs[:-4], refs[-4:-1], refs[-1]
    sub, wide = pieces[0].shape
    hid = weights[0].shape[1]
    for i, piece in enumerate(pieces):
        out[i * sub : (i + 1) * sub, :wide] = piece[...]
    for i, weight in enumerate(weights):
        out[:, wide + i * hid : wide + (i + 1) * hid] = weight[...]


def fetch(bundles, columns, held, sems):
    copies = [
        pltpu.make_async_copy(bundle.at[:, columns], held.at[i], sems.at[i])
        for i, bundle in enumerate(bundles)
    ]
    for copy in copies:
        copy.start()
    for copy in copies:
        copy.wait()


def weights_at(parts, distance, position, width, held):
    per_half = parts // 2
    source = source_of(parts, position, distance)
    of = pl.ds(pl.multiple_of(lax.rem(source, per_half) * width, width), width)
    return held[jnp.where(source // per_half == position[1], 0, 1), of, :]


def forward_most(parts, distances, middle, position, *refs):
    xs, dys = refs[: len(distances)], refs[len(distances) : 2 * len(distances)]
    own_bundle, other_bundle, out, mid_ref, held, sems = refs[2 * len(distances) :]
    rows, width = xs[0].shape
    hid = out.shape[1] // 3
    fetch((own_bundle, other_bundle), pl.ds(2 * hid, 3 * hid), held, sems)
    acc, back = jnp.zeros((rows, 2 * hid), F32), jnp.zeros((rows, hid), F32)
    for d, x, dy in zip(distances, xs, dys):
        piece = weights_at(parts, d, position, width, held)
        acc = acc + jnp.dot(x[...], piece[:, : 2 * hid], preferred_element_type=F32)
        back = back + jnp.dot(dy[...], piece[:, 2 * hid :], preferred_element_type=F32)
    out[:, : 2 * hid] = acc
    out[:, 2 * hid :] = back
    mid_ref[...] = weights_at(parts, middle, position, width, held)


def forward_last(_, x_ref, dy_ref, piece_ref, begun, both_ref, hidden_ref):
    hid = hidden_ref.shape[1]
    acc = begun[:, : 2 * hid] + jnp.dot(
        x_ref[...], piece_ref[:, : 2 * hid], preferred_element_type=F32
    )
    back = begun[:, 2 * hid :] + jnp.dot(
        dy_ref[...], piece_ref[:, 2 * hid :], preferred_element_type=F32
    )
    gate, up = acc[:, :hid], acc[:, hid:]
    sig = 1.0 / (1.0 + jnp.exp(-gate))
    act = gate * sig
    hidden_ref[...] = (act * up).astype(BF16)
    both_ref[:, :hid] = (back * up * sig * (1.0 + gate * (1.0 - sig))).astype(BF16)
    both_ref[:, hid:] = (back * act).astype(BF16)


def back_kernel(parts, capacity, position, *refs):
    blocks, (own_bundle, other_bundle, out_ref, flat, held, sems) = refs[:parts], refs[parts:]
    fetch((own_bundle, other_bundle), pl.ds(0, held.shape[2]), held, sems)
    place, core = position[0], position[1]
    per_half = parts // 2
    sub = held.shape[1] // parts
    rows, width = blocks[0].shape[0], 2 * sub
    owners, chunks = rows // capacity, width // LANES
    stretch = flat.shape[0] // owners
    ahead = lax.rem(core + place // per_half, 2)
    own, other = jnp.zeros((rows, sub), F32), jnp.zeros((rows, sub), F32)
    contract = (((1,), (1,)), ((), ()))
    for d in range(parts):
        block = blocks[d][...]
        at = pl.multiple_of(lax.rem(position[2] * d + parts + per_half * ahead, parts) * sub, sub)
        own = own + lax.dot_general(
            block, held[0, pl.ds(at, sub), :], contract, preferred_element_type=F32
        )
        at = pl.multiple_of(lax.rem(position[2] * d + parts + per_half * (1 - ahead), parts) * sub, sub)
        other = other + lax.dot_general(
            block, held[1, pl.ds(at, sub), :], contract, preferred_element_type=F32
        )
    first = core == 0
    total = jnp.concatenate((jnp.where(first, own, other), jnp.where(first, other, own)), axis=1)
    for s in range(capacity):
        for c in range(chunks):
            flat[pl.ds(s * chunks + c, owners, stride=stretch), :] = total[
                s * owners : (s + 1) * owners, c * LANES : (c + 1) * LANES
            ]
    for pad in range(capacity * chunks, stretch):
        flat[pl.ds(pad, owners, stride=stretch), :] = jnp.zeros((owners, LANES), F32)
    out_ref[...] = flat[...].astype(BF16)


def combine_kernel(capacity, _, flat_ref, table_far, out_ref, flat, rows_ref, table, sem):
    copy = pltpu.make_async_copy(table_far, table, sem)
    copy.start()
    rows, width = rows_ref.shape
    owners, chunks = rows // capacity, width // LANES
    stretch = flat.shape[0] // owners
    flat[...] = flat_ref[...].astype(F32)
    for s in range(capacity):
        for c in range(chunks):
            rows_ref[s * owners : (s + 1) * owners, c * LANES : (c + 1) * LANES] = flat[
                pl.ds(s * chunks + c, owners, stride=stretch), :
            ].astype(BF16)
    copy.wait()
    out_ref[...] = transposed_dot(table[...], rows_ref[...]).astype(BF16)


def grads_kernel(parts, position, *refs):
    xs, dys, both_ref, hidden_ref = refs[:parts], refs[parts : 2 * parts], *refs[2 * parts :][:2]
    rest = refs[2 * parts + 2 :]
    wanted = position[1]
    width = xs[0].shape[1]
    hid = hidden_ref.shape[1]
    per_half = parts // 2
    for d in range(parts):
        source = source_of(parts, position, d)

        @pl.when(source // per_half == wanted)
        def _():
            into = pl.ds(pl.multiple_of(lax.rem(source, per_half) * width, width), width)
            both = transposed_dot(xs[d][...], both_ref[...]).astype(BF16)
            down = transposed_dot(dys[d][...], hidden_ref[...]).astype(BF16)
            for i, share in enumerate((both[:, :hid], both[:, hid:], down)):
                if len(rest) > 3:
                    more = rest[i][0, into, :].astype(F32)
                    share = (share.astype(F32) + more).astype(BF16)
                rest[i - 3][0, into, :] = share


def grads(position, which, operands, outs):
    xs, dys, both, hidden, *received = operands
    parts = len(xs)
    half = parts // 2 * xs[0].shape[1]
    return local_call(
        lambda *refs: grads_kernel(parts, *refs),
        "grads",
        position.at[1].set(which),
        (*xs, *dys, both, hidden, *received),
        outs,
        flops=2 * both.shape[0] * half * (both.shape[1] + hidden.shape[1]),
        vmem=56,
    )


def shards(tokens, cotangent, expert_ids, probs, gate_weight, up_weight, down_weight):
    peers = ("x", "z")
    owners = lax.axis_size("x") * lax.axis_size("z")
    parts = lax.axis_size("y")
    core, place = lax.axis_index("dp"), lax.axis_index("y")
    tok, model = tokens.shape
    choose = expert_ids.shape[1]
    width = model // parts
    chunks = width // LANES
    hid = gate_weight.shape[2]
    capacity = min(tok, (5 * tok * choose + 4 * owners - 1) // (4 * owners))
    rows = owners * capacity
    half = parts // 2
    swap = [(0, 1), (1, 0)]
    place, core = place.astype(jnp.int32), core.astype(jnp.int32)
    position = jnp.stack((place, core, 1 - 2 * core))

    flat, table = pack(
        expert_ids.T, probs.T, tokens, cotangent, place[None], width, owners, capacity
    )
    flat, own_weights = lax.optimization_barrier(
        (flat, (gate_weight[0], up_weight[0], down_weight[0]))
    )
    flat = lax.all_to_all(
        flat.reshape(owners, -1, LANES), peers, split_axis=0, concat_axis=0, tiled=True
    )
    sub = width // 2
    turned = [None] * parts
    for k in reversed(range(parts)):
        target = lax.rem(place + k, parts)
        start = lax.rem(target, half) * width + target // half * sub
        piece = jnp.concatenate(
            [lax.dynamic_slice_in_dim(w, start, sub, 0) for w in own_weights[:2]], axis=1
        )
        perm = []
        for h in range(2):
            for p in range(parts):
                t = (p + k) % parts
                perm.append((h * parts + p, t // half * parts + h * half + t % half))
        turned[k] = lax.ppermute(piece, ("dp", "y"), perm)
    flat, turned = lax.optimization_barrier((flat, turned[::-1]))
    turned = turned[::-1]
    bundle = local_call(
        bundle_kernel,
        "bundle",
        position,
        (*turned, *own_weights),
        jax.ShapeDtypeStruct((model // 2, 5 * hid), BF16),
    )
    bundles = (bundle, lax.ppermute(bundle, "dp", swap))
    flat = flat.reshape(-1, LANES)
    pair = jax.ShapeDtypeStruct((rows, width), BF16)
    own = local_call(
        lambda *refs: unpack_kernel(capacity, *refs),
        "unpack",
        position,
        (flat,),
        (pair, pair),
        [pltpu.VMEM(flat.shape, F32)],
    )

    def ring(value, rightward, axes, on, back):
        held = {0: value}
        right = left = value
        for d in range(1, half + 1):
            if d < half or rightward:
                right = lax.ppermute(right, axes, on)
                held[d] = right
            if d < half or not rightward:
                left = lax.ppermute(left, axes, back)
                held[parts - d] = left
        return [held[d] for d in range(parts)]

    two_way = ("dp", "y"), around(parts, 1), around(parts, -1)
    xs, dys = ring(own[0], True, *two_way), ring(own[1], False, *two_way)
    most = [d for d in range(parts) if d != half]
    begun, piece = local_call(
        lambda *refs: forward_most(parts, most, half, *refs),
        "forward_most",
        position,
        (*[xs[d] for d in most], *[dys[d] for d in most]),
        (
            jax.ShapeDtypeStruct((rows, 3 * hid), F32),
            jax.ShapeDtypeStruct((width, 3 * hid), BF16),
        ),
        [pltpu.VMEM((2, model // 2, 3 * hid), BF16), pltpu.SemaphoreType.DMA((2,))],
        flops=2 * rows * model * 3 * hid,
        far=bundles,
    )
    d_both, hidden = local_call(
        forward_last,
        "forward_last",
        position,
        (xs[half], dys[half], piece, begun),
        (
            jax.ShapeDtypeStruct((rows, 2 * hid), BF16),
            jax.ShapeDtypeStruct((rows, hid), BF16),
        ),
        flops=2 * rows * width * 3 * hid,
    )

    stretch = -(-capacity * chunks // TILE) * TILE
    d_rows = local_call(
        lambda *refs: back_kernel(parts, capacity, *refs),
        "back",
        position.at[2].set(1),
        ring(d_both, True, "y", shift(parts, 1), shift(parts, -1)),
        jax.ShapeDtypeStruct((owners * stretch, LANES), BF16),
        [
            pltpu.VMEM((owners * stretch, LANES), F32),
            pltpu.VMEM((2, model // 2, 2 * hid), BF16),
            pltpu.SemaphoreType.DMA((2,)),
        ],
        flops=4 * rows * width * parts * hid,
        far=bundles,
    )
    d_rows, operands = lax.optimization_barrier((d_rows, (xs, dys, d_both, hidden)))
    returned = lax.all_to_all(
        d_rows.reshape(owners, -1, LANES), peers, split_axis=0, concat_axis=0, tiled=True
    )
    outs = (jax.ShapeDtypeStruct(gate_weight.shape, BF16),) * 3
    received = [
        lax.ppermute(share, "dp", swap) for share in grads(position, 1 - core, operands, outs)
    ]
    final = grads(position, core, (*operands, *received), outs)
    returned, final = lax.optimization_barrier((returned, final))
    d_tokens = local_call(
        lambda *refs: combine_kernel(capacity, *refs),
        "combine",
        position,
        (returned.reshape(-1, LANES),),
        jax.ShapeDtypeStruct((tok, width), BF16),
        [
            pltpu.VMEM((owners * stretch, LANES), F32),
            pltpu.VMEM((rows, width), BF16),
            pltpu.VMEM(table.shape, BF16),
            pltpu.SemaphoreType.DMA(()),
        ],
        far=(table,),
        vmem=60,
    )
    return d_tokens, *final


def solution(mesh):
    dp, experts, etp = mesh.devices.shape
    inner = min(16, experts)
    grid = Mesh(mesh.devices.reshape(dp, experts // inner, inner, etp), ("dp", "x", "z", "y"))
    row = P(("dp", "x", "z"), None)
    weight = P(("x", "z"), "dp", "y")
    return jax.shard_map(
        shards,
        mesh=grid,
        in_specs=(row, row, row, row, weight, weight, weight),
        out_specs=(P(("dp", "x", "z"), "y"), weight, weight, weight),
        check_vma=False,
    )
```
